512 devices in a mesh: expert: 64 (over y_hi, z, x), fsdp: 8 (over y_lo, core).
Axes of the slice: x: 4, y: 8 (y_hi: 2, y_lo: 4; y = y_hi * 4 + y_lo), z: 8, core: 2. Of those that a mesh axis runs over, the one named last changes fastest.
Arguments:
- expert_weights: bfloat16 [64, 7168, 1024], P(None, 'expert', 'fsdp'), may hold values from -0.0625 to 0.0625
- kv_up_weight: bfloat16 [512, 32768], P('fsdp', 'expert'), may hold values from -8 to 8
- owner_table: int32 [256], replicated, may hold values from 0 to 63, as said below
- moved_experts: int32 [64], replicated, may hold values from 0 to 255, as said below
Outputs:
- expert_values: bfloat16 [64, 7168, 1024], P('expert', None, 'fsdp')
- expert_scales: float32 [64, 56, 8], P('expert', None, 'fsdp')
- mla_values: bfloat16 [512, 32768], P(None, 'expert')
- mla_scales: float32 [4, 256], P(None, 'expert')
The draws below stay inside these ranges and needn't reach their ends.
Inputs may be any that keep to these rules, and one draw needn't show every extreme that they name: For every owner i from 0 to 63, exactly 1 of the experts named in moved_experts have owner_table value i; other entries are any owner. `moved_experts`: distinct layer expert numbers.
All inputs are finite; a program needn't handle non-finite values.
Results may differ from the reference program's by a relative error of at most 0.0045.
Values may be sent and summed in bfloat16 or wider, within the bound.
A program may use at most 64 MiB of HBM per device.

```python
import jax
import jax.numpy as jnp
from jax import lax

D = 7168
GLOBAL_EXPERTS = 256
KV_RANK = 512
MLA_COLS = 32768
FFW = 1024
BLOCK = 128
EXP_DEV = 1
EXPERTS = 64
N_EXPERT = 64


def shared_tables(key):
    shuffled = jax.random.permutation(jax.random.fold_in(key, 101), GLOBAL_EXPERTS - 1)
    placing = jax.random.permutation(jax.random.fold_in(key, 102), EXPERTS)
    mixing = jax.random.permutation(jax.random.fold_in(key, 104), EXPERTS)
    chosen = jnp.concatenate([shuffled[:EXPERTS - 1].astype(jnp.int32), jnp.full((1,), GLOBAL_EXPERTS - 1, jnp.int32)])
    picked = jnp.take(chosen, mixing).astype(jnp.int32)
    others = jax.random.randint(jax.random.fold_in(key, 103), (GLOBAL_EXPERTS,), 0, N_EXPERT).astype(jnp.int32)
    lookup = others.at[picked].set((placing // EXP_DEV).astype(jnp.int32))
    return (lookup.astype(jnp.int32), picked)


def draw_owner_table(key, part):
    shared = shared_tables(key)
    return shared[0]


def draw_moved_experts(key, part):
    shared = shared_tables(key)
    return shared[1]


def draw_kv_up_weight(key, part):
    key = jax.random.fold_in(key, 5)
    row_key = jax.random.fold_in(key, 11)
    col_key = jax.random.fold_in(key, 12)
    base_key = jax.random.fold_in(key, 13)
    row_scale = jnp.exp(jax.random.uniform(row_key, (KV_RANK, 1), jnp.float32, 0.0, 2.302585))
    col_scale = jnp.exp(jax.random.uniform(col_key, (1, MLA_COLS), jnp.float32, 0.0, 2.302585))
    base = jax.random.truncated_normal(base_key, -4.0, 4.0, (KV_RANK, MLA_COLS), jnp.float32)
    return (0.02 * base * row_scale * col_scale).astype(jnp.bfloat16)


def block_levels(own_key, dims, shards, least, high):
    level, own = 1.0, jax.random.fold_in(own_key, 6)
    for dim, blocks in shards:
        heights = jnp.exp(jax.random.uniform(jax.random.fold_in(own, dim), (blocks,), jnp.float32, least / len(shards), high / len(shards)))
        level = level * jnp.repeat(heights, dims[dim] // blocks).reshape([-1 if axis == dim else 1 for axis in range(len(dims))])
    return level


def scatter_about(rng, dims, deviation, bound, pieces=(), kind=jnp.bfloat16):
    gain = block_levels(rng, dims, pieces, -0.22, 0.18) if pieces else 1.0
    values = jax.random.normal(rng, dims, jnp.float32) * deviation * gain
    return jnp.minimum(jnp.maximum(values, -bound), bound).astype(kind)


def setup_inputs(seed: int = 0) -> dict:
    arg_keys = jax.random.split(jax.random.key(seed), 5)
    return {
        "expert_weights": scatter_about(arg_keys[0], (EXPERTS, D, FFW), D ** -0.5, 0.0625, ((1, 64), (2, 8))),
        "kv_up_weight": draw_kv_up_weight(jax.random.fold_in(arg_keys[4], 71), 0),
        "owner_table": draw_owner_table(jax.random.fold_in(arg_keys[4], 71), 0),
        "moved_experts": draw_moved_experts(jax.random.fold_in(arg_keys[4], 71), 0),
    }


EPSILON = 1e-6


def block_maxima(values, row_block, col_block):
    dims_in = values.shape
    folded = jnp.abs(values).reshape(dims_in[:-2] + (dims_in[-2] // row_block, row_block, dims_in[-1] // col_block, col_block))
    return jnp.max(folded, axis=(-3, -1))


def divide_blocks(values, scales, row_block, col_block):
    dims_in = values.shape
    folded = values.reshape(dims_in[:-2] + (dims_in[-2] // row_block, row_block, dims_in[-1] // col_block, col_block))
    return (folded / scales[..., :, None, :, None]).reshape(dims_in).astype(jnp.bfloat16)


def requantize(values, row_block, col_block):
    scales = block_maxima(values, row_block, col_block) + EPSILON
    return divide_blocks(values, scales, row_block, col_block), scales


def per_expert(matrix):
    return requantize(matrix.astype(jnp.float32), BLOCK, BLOCK)


def reference(expert_weights, kv_up_weight, owner_table, moved_experts):
    owners = jnp.take(owner_table, moved_experts).astype(jnp.int32)
    sort_keys = owners * EXPERTS + jnp.arange(EXPERTS).astype(jnp.int32)
    ranking = jnp.argsort(sort_keys).astype(jnp.int32)
    ordered = jnp.take(expert_weights, ranking, axis=0)
    expert_values, expert_scales = lax.map(per_expert, ordered)
    mla_values, mla_scales = requantize(kv_up_weight.astype(jnp.float32), BLOCK, BLOCK)
    return (expert_values, expert_scales, mla_values, mla_scales)
```

```python
import functools

import jax
import jax.numpy as jnp
from jax import lax
from jax.experimental import pallas as pl
from jax.experimental.pallas import tpu as pltpu
from jax.sharding import PartitionSpec as P

MESH = pl.DeviceIdType.MESH
BLOCK = 128
EPSILON = 1e-06
Y_HI, Z, X = 2, 8, 4
Y_LO, CORE = 4, 2
RING_LINKS = ("y+", "y-", "z+", "z-", "x+", "x-")


def link_loads(offset):
    dy, dz, dx = offset
    loads = dict.fromkeys(RING_LINKS, 0)
    if dy:
        loads["y+"] = loads["y-"] = 2
    if dz == Z // 2:
        loads["z+"] = loads["z-"] = 2
    elif dz:
        loads["z+" if dz < Z // 2 else "z-"] = min(dz, Z - dz)
    if dx == X // 2:
        loads["x+"] = loads["x-"] = 1
    elif dx:
        loads["x+" if dx < X // 2 else "x-"] = 1
    return loads


def balanced_order():
    rest = [(dy, dz, dx) for dy in range(Y_HI) for dz in range(Z) for dx in range(X)][1:]
    count = len(rest)
    total = {k: sum(link_loads(o)[k] for o in rest) for k in RING_LINKS}
    done, order = dict.fromkeys(RING_LINKS, 0), []
    while rest:
        share = (len(order) + 1) / count

        def cost(offset):
            loads = link_loads(offset)
            return sum(
                (done[k] + loads[k] - total[k] * share) ** 2 * (0.3 if k[0] == "x" else 1.0)
                for k in RING_LINKS
            )

        best = min(rest, key=cost)
        rest.remove(best)
        order.append(best)
        for k, v in link_loads(best).items():
            done[k] += v
    return order


ORDER = balanced_order()


def kernel(
    x_hbm, kv_hbm, table_ref, moved_ref,
    values_ref, scales_ref, mla_values_ref, mla_scales_ref,
    x_ref, staged, landed, kv_landed, rank_vmem, rank_smem,
    in_sem, send_sem, recv_sem, kv_send, kv_recv, rank_sem,
):
    n = Y_HI * Z * X
    rows = x_ref.shape[1]
    me, fs = lax.axis_index("expert"), lax.axis_index("fsdp")
    y_hi, z, x = me // (Z * X), (me // X) % Z, me % X
    y_lo, core = fs // CORE, fs % CORE

    load_x = pltpu.make_async_copy(x_hbm, x_ref, in_sem.at[0])
    load_x.start()
    kv_rows = kv_hbm.shape[0]
    my_kv = kv_landed.at[pl.ds(pl.multiple_of(fs * kv_rows, kv_rows), kv_rows)]
    load_kv = pltpu.make_async_copy(kv_hbm, my_kv, in_sem.at[1])
    load_kv.start()

    ys = [((y_hi + d) % Y_HI) * (Z * X) for d in range(Y_HI)]
    zs = [((z + d) % Z) * X for d in range(Z)]
    xs = [(x + d) % X for d in range(X)]

    def peer(offset):
        return ys[offset[0]] + zs[offset[1]] + xs[offset[2]]

    def negative(offset):
        return (-offset[0] % Y_HI, -offset[1] % Z, -offset[2] % X)

    fs_same = [((y_lo + d) % Y_LO) * CORE + core for d in range(Y_LO)]
    sibling = y_lo * CORE + 1 - core

    barrier = pltpu.get_barrier_semaphore()
    for offset in ORDER:
        pl.semaphore_signal(barrier, inc=1, device_id=(peer(negative(offset)), fs), device_id_type=MESH)
    for d in range(1, Y_LO):
        pl.semaphore_signal(barrier, inc=1, device_id=(me, fs_same[d]), device_id_type=MESH)
    pl.semaphore_signal(barrier, inc=1, device_id=(me, sibling), device_id_type=MESH)

    lane = lax.broadcasted_iota(jnp.int32, (n, n), 1)
    row = lax.broadcasted_iota(jnp.int32, (n, n), 0)
    moved = jnp.sum(jnp.where(lane == row, moved_ref[...], 0), axis=1, keepdims=True)
    layer = lax.broadcasted_iota(jnp.int32, (n, table_ref.shape[1]), 1)
    owners = jnp.sum(jnp.where(layer == moved, table_ref[...], 0), axis=1, keepdims=True)
    wide = lax.broadcasted_iota(jnp.int32, (n, 128), 1)
    position = lax.broadcasted_iota(jnp.int32, (n, 128), 0)
    ranking = jnp.max(jnp.where(owners == wide, position, 0), axis=0, keepdims=True)
    rank_vmem[...] = jnp.broadcast_to(ranking, rank_vmem.shape)
    to_smem = pltpu.make_async_copy(rank_vmem, rank_smem, rank_sem)
    to_smem.start()
    to_smem.wait()
    load_x.wait()
    load_kv.wait()

    pl.semaphore_wait(barrier, len(ORDER) + Y_LO)

    def kv_copy(source, target, dev):
        part = kv_landed.at[pl.ds(pl.multiple_of(source * kv_rows, kv_rows), kv_rows)]
        return pltpu.make_async_remote_copy(
            src_ref=part, dst_ref=part, send_sem=kv_send.at[target], recv_sem=kv_recv.at[source],
            device_id=(me, dev), device_id_type=MESH,
        )

    kv_out = [kv_copy(fs, 0, sibling)] + [kv_copy(fs, d, fs_same[d]) for d in range(1, Y_LO)]

    my_rows = pl.ds(pl.multiple_of(me * rows, 16), rows)
    for i, offset in enumerate(ORDER):
        dest = peer(offset)
        part = pl.ds(i * rows, rows)
        staged[part, :] = x_ref[rank_smem[0, dest]]
        pltpu.make_async_remote_copy(
            src_ref=staged.at[part], dst_ref=landed.at[my_rows], send_sem=send_sem,
            recv_sem=recv_sem.at[me], device_id=(dest, fs), device_id_type=MESH,
        ).start()
        if i == 3:
            for copy in kv_out:
                copy.start()
    landed[my_rows, :] = x_ref[rank_smem[0, me]]

    kv_relay = []
    for d in range(1, Y_LO):
        source = fs_same[d]
        kv_copy(source, 0, fs_same[d]).wait_recv()
        copy = kv_copy(source, Y_LO - 1 + d, sibling)
        copy.start()
        kv_relay.append(copy)
    for d in range(Y_LO):
        source = ((y_lo + d) % Y_LO) * CORE + 1 - core
        kv_copy(source, 0, sibling).wait_recv()

    def scaled(block):
        block = block.astype(jnp.float32)
        top = jnp.max(jnp.max(jnp.abs(block), axis=0, keepdims=True), axis=1, keepdims=True)
        scale = top + EPSILON
        return (block * (1.0 / scale)).astype(jnp.bfloat16), scale

    tall, across = mla_scales_ref.shape
    at = lax.broadcasted_iota(jnp.int32, (tall, across), 0) * across + lax.broadcasted_iota(jnp.int32, (tall, across), 1)
    mla_scales = jnp.zeros((tall, across), jnp.float32)
    for a in range(tall):
        for b in range(across):
            where = (pl.ds(a * BLOCK, BLOCK), pl.ds(b * BLOCK, BLOCK))
            mla_values_ref[where], scale = scaled(kv_landed[where])
            mla_scales = jnp.where(at == a * across + b, scale, mla_scales)
    mla_scales_ref[...] = mla_scales

    group, blocks = 8, 8 * rows // BLOCK
    slots = lax.broadcasted_iota(jnp.int32, scales_ref.shape, 1)

    def one_group(g, scales):
        for s in range(group):
            source = g * group + s

            @pl.when(source != me)
            def _():
                where = pl.ds(pl.multiple_of(source * rows, 16), rows)
                pltpu.make_async_remote_copy(
                    src_ref=landed.at[where], dst_ref=landed.at[where], send_sem=send_sem,
                    recv_sem=recv_sem.at[source], device_id=(source, fs), device_id_type=MESH,
                ).wait_recv()

        for b in range(blocks):
            where = pl.ds(pl.multiple_of((g * blocks + b) * BLOCK, BLOCK), BLOCK)
            values_ref[where, :], scale = scaled(landed[where, :])
            scales = jnp.where(slots == g * blocks + b, scale, scales)
        return scales

    scales_ref[...] = lax.fori_loop(0, n // group, one_group, jnp.zeros(scales_ref.shape, jnp.float32))

    sent = staged.at[pl.ds(0, len(ORDER) * rows)]
    pltpu.make_async_remote_copy(
        src_ref=sent, dst_ref=sent, send_sem=send_sem, recv_sem=recv_sem.at[me],
        device_id=(peer(ORDER[0]), fs), device_id_type=MESH,
    ).wait_send()
    for copy in kv_out + kv_relay:
        copy.wait_send()


def on_device(expert_weights, kv_up_weight, owner_table, moved_experts):
    n, rows, columns = expert_weights.shape
    kv_rows, kv_columns = kv_up_weight.shape
    kv_all = kv_rows * Y_LO * CORE
    whole = n * rows
    vmem = pl.BlockSpec(memory_space=pltpu.VMEM)
    anywhere = pl.BlockSpec(memory_space=pl.ANY)
    values, scales, mla_values, mla_scales = pl.pallas_call(
        kernel,
        out_shape=(
            jax.ShapeDtypeStruct((whole, columns), jnp.bfloat16),
            jax.ShapeDtypeStruct((1, whole // BLOCK), jnp.float32),
            jax.ShapeDtypeStruct((kv_all, kv_columns), jnp.bfloat16),
            jax.ShapeDtypeStruct((kv_all // BLOCK, kv_columns // BLOCK), jnp.float32),
        ),
        in_specs=[anywhere, anywhere, vmem, vmem],
        out_specs=(vmem, vmem, vmem, vmem),
        scratch_shapes=[
            pltpu.VMEM((n, rows, columns), jnp.bfloat16),
            pltpu.VMEM((whole, columns), jnp.bfloat16),
            pltpu.VMEM((whole, columns), jnp.bfloat16),
            pltpu.VMEM((kv_all, kv_columns), jnp.bfloat16),
            pltpu.VMEM((8, 128), jnp.int32),
            pltpu.SMEM((8, 128), jnp.int32),
            pltpu.SemaphoreType.DMA((2,)),
            pltpu.SemaphoreType.DMA,
            pltpu.SemaphoreType.DMA((n,)),
            pltpu.SemaphoreType.DMA((2 * Y_LO,)),
            pltpu.SemaphoreType.DMA((Y_LO * CORE,)),
            pltpu.SemaphoreType.DMA,
        ],
        compiler_params=pltpu.CompilerParams(
            collective_id=0, has_side_effects=True, vmem_limit_bytes=40 << 20
        ),
    )(
        expert_weights, kv_up_weight,
        owner_table.reshape(1, -1), moved_experts.reshape(1, -1),
    )
    return (
        values.reshape(1, whole, columns),
        scales.reshape(1, whole // BLOCK, 1),
        mla_values,
        mla_scales,
    )


def solution(mesh):
    in_specs = (P(None, "expert", "fsdp"), P("fsdp", "expert"), P(), P())
    out_specs = (
        P("expert", None, "fsdp"),
        P("expert", None, "fsdp"),
        P(None, "expert"),
        P(None, "expert"),
    )
    return jax.shard_map(
        on_device, mesh=mesh, in_specs=in_specs, out_specs=out_specs, check_vma=False
    )
```

```python
import functools

import jax
import jax.numpy as jnp
from jax import lax
from jax.experimental import pallas as pl
from jax.experimental.pallas import tpu as pltpu
from jax.sharding import PartitionSpec as P

MESH = pl.DeviceIdType.MESH
BLOCK = 128
EPSILON = 1e-06
Y_HI, Z, X = 2, 8, 4
Y_LO, CORE = 4, 2
RING_LINKS = ("y+", "y-", "z+", "z-", "x+", "x-")


def link_loads(offset):
    dy, dz, dx = offset
    loads = dict.fromkeys(RING_LINKS, 0)
    if dy:
        loads["y+"] = loads["y-"] = 2
    if dz == Z // 2:
        loads["z+"] = loads["z-"] = 2
    elif dz:
        loads["z+" if dz < Z // 2 else "z-"] = min(dz, Z - dz)
    if dx == X // 2:
        loads["x+"] = loads["x-"] = 1
    elif dx:
        loads["x+" if dx < X // 2 else "x-"] = 1
    return loads


def balanced_order():
    rest = [(dy, dz, dx) for dy in range(Y_HI) for dz in range(Z) for dx in range(X)][1:]
    count = len(rest)
    total = {k: sum(link_loads(o)[k] for o in rest) for k in RING_LINKS}
    done, order = dict.fromkeys(RING_LINKS, 0), []
    while rest:
        share = (len(order) + 1) / count

        def cost(offset):
            loads = link_loads(offset)
            return sum(
                (done[k] + loads[k] - total[k] * share) ** 2 * (0.3 if k[0] == "x" else 1.0)
                for k in RING_LINKS
            )

        best = min(rest, key=cost)
        rest.remove(best)
        order.append(best)
        for k, v in link_loads(best).items():
            done[k] += v
    return order


ORDER = balanced_order()


def kernel(
    x_hbm, kv_hbm, table_hbm, moved_hbm,
    values_ref, scales_ref, mla_values_ref, mla_scales_ref,
    x_ref, staged, landed, kv_landed, table_ref, moved_ref, rank_vmem, rank_smem,
    in_sem, send_sem, recv_sem, kv_send, kv_recv, rank_sem,
):
    n = Y_HI * Z * X
    rows = x_ref.shape[1]
    me, fs = lax.axis_index("expert"), lax.axis_index("fsdp")
    y_hi, z, x = me // (Z * X), (me // X) % Z, me % X
    y_lo, core = fs // CORE, fs % CORE

    load_moved = pltpu.make_async_copy(moved_hbm, moved_ref, in_sem.at[2])
    load_moved.start()
    load_table = pltpu.make_async_copy(table_hbm, table_ref, in_sem.at[3])
    load_table.start()
    load_x = pltpu.make_async_copy(x_hbm, x_ref, in_sem.at[0])
    load_x.start()
    kv_rows = kv_hbm.shape[0]
    my_kv = kv_landed.at[pl.ds(pl.multiple_of(fs * kv_rows, kv_rows), kv_rows)]
    load_kv = pltpu.make_async_copy(kv_hbm, my_kv, in_sem.at[1])
    load_kv.start()

    ys = [((y_hi + d) % Y_HI) * (Z * X) for d in range(Y_HI)]
    zs = [((z + d) % Z) * X for d in range(Z)]
    xs = [(x + d) % X for d in range(X)]

    def peer(offset):
        return ys[offset[0]] + zs[offset[1]] + xs[offset[2]]

    def negative(offset):
        return (-offset[0] % Y_HI, -offset[1] % Z, -offset[2] % X)

    fs_same = [((y_lo + d) % Y_LO) * CORE + core for d in range(Y_LO)]
    sibling = y_lo * CORE + 1 - core

    barrier = pltpu.get_barrier_semaphore()
    for offset in ORDER:
        pl.semaphore_signal(barrier, inc=1, device_id=(peer(negative(offset)), fs), device_id_type=MESH)
    for d in range(1, Y_LO):
        pl.semaphore_signal(barrier, inc=1, device_id=(me, fs_same[d]), device_id_type=MESH)
    pl.semaphore_signal(barrier, inc=1, device_id=(me, sibling), device_id_type=MESH)

    load_moved.wait()
    load_table.wait()
    lane = lax.broadcasted_iota(jnp.int32, (n, n), 1)
    row = lax.broadcasted_iota(jnp.int32, (n, n), 0)
    moved = jnp.sum(jnp.where(lane == row, moved_ref[...], 0), axis=1, keepdims=True)
    layer = lax.broadcasted_iota(jnp.int32, (n, table_ref.shape[1]), 1)
    owners = jnp.sum(jnp.where(layer == moved, table_ref[...], 0), axis=1, keepdims=True)
    wide = lax.broadcasted_iota(jnp.int32, (n, 128), 1)
    position = lax.broadcasted_iota(jnp.int32, (n, 128), 0)
    ranking = jnp.max(jnp.where(owners == wide, position, 0), axis=0, keepdims=True)
    rank_vmem[...] = jnp.broadcast_to(ranking, rank_vmem.shape)
    to_smem = pltpu.make_async_copy(rank_vmem, rank_smem, rank_sem)
    to_smem.start()
    to_smem.wait()
    load_x.wait()
    load_kv.wait()

    pl.semaphore_wait(barrier, len(ORDER) + Y_LO)

    def kv_copy(source, target, dev):
        part = kv_landed.at[pl.ds(pl.multiple_of(source * kv_rows, kv_rows), kv_rows)]
        return pltpu.make_async_remote_copy(
            src_ref=part, dst_ref=part, send_sem=kv_send.at[target], recv_sem=kv_recv.at[source],
            device_id=(me, dev), device_id_type=MESH,
        )

    kv_out = [kv_copy(fs, 0, sibling)] + [kv_copy(fs, d, fs_same[d]) for d in range(1, Y_LO)]

    my_rows = pl.ds(pl.multiple_of(me * rows, 16), rows)
    for i, offset in enumerate(ORDER):
        dest = peer(offset)
        part = pl.ds(i * rows, rows)
        staged[part, :] = x_ref[rank_smem[0, dest]]
        pltpu.make_async_remote_copy(
            src_ref=staged.at[part], dst_ref=landed.at[my_rows], send_sem=send_sem,
            recv_sem=recv_sem.at[me], device_id=(dest, fs), device_id_type=MESH,
        ).start()
        if i == 3:
            for copy in kv_out:
                copy.start()
    landed[my_rows, :] = x_ref[rank_smem[0, me]]

    kv_relay = []
    for d in range(1, Y_LO):
        source = fs_same[d]
        kv_copy(source, 0, fs_same[d]).wait_recv()
        copy = kv_copy(source, Y_LO - 1 + d, sibling)
        copy.start()
        kv_relay.append(copy)
    for d in range(Y_LO):
        source = ((y_lo + d) % Y_LO) * CORE + 1 - core
        kv_copy(source, 0, sibling).wait_recv()

    def scaled(block):
        block = block.astype(jnp.float32)
        top = jnp.max(jnp.max(jnp.abs(block), axis=0, keepdims=True), axis=1, keepdims=True)
        scale = top + EPSILON
        return (block * (1.0 / scale)).astype(jnp.bfloat16), scale

    tall, across = mla_scales_ref.shape
    at = lax.broadcasted_iota(jnp.int32, (tall, across), 0) * across + lax.broadcasted_iota(jnp.int32, (tall, across), 1)
    mla_scales = jnp.zeros((tall, across), jnp.float32)
    for a in range(tall):
        for b in range(across):
            where = (pl.ds(a * BLOCK, BLOCK), pl.ds(b * BLOCK, BLOCK))
            mla_values_ref[where], scale = scaled(kv_landed[where])
            mla_scales = jnp.where(at == a * across + b, scale, mla_scales)
    mla_scales_ref[...] = mla_scales

    group, blocks = 8, 8 * rows // BLOCK
    slots = lax.broadcasted_iota(jnp.int32, scales_ref.shape, 1)

    def one_group(g, scales):
        for s in range(group):
            source = g * group + s

            @pl.when(source != me)
            def _():
                where = pl.ds(pl.multiple_of(source * rows, 16), rows)
                pltpu.make_async_remote_copy(
                    src_ref=landed.at[where], dst_ref=landed.at[where], send_sem=send_sem,
                    recv_sem=recv_sem.at[source], device_id=(source, fs), device_id_type=MESH,
                ).wait_recv()

        for b in range(blocks):
            where = pl.ds(pl.multiple_of((g * blocks + b) * BLOCK, BLOCK), BLOCK)
            values_ref[where, :], scale = scaled(landed[where, :])
            scales = jnp.where(slots == g * blocks + b, scale, scales)
        return scales

    scales_ref[...] = lax.fori_loop(0, n // group, one_group, jnp.zeros(scales_ref.shape, jnp.float32))

    sent = staged.at[pl.ds(0, len(ORDER) * rows)]
    pltpu.make_async_remote_copy(
        src_ref=sent, dst_ref=sent, send_sem=send_sem, recv_sem=recv_sem.at[me],
        device_id=(peer(ORDER[0]), fs), device_id_type=MESH,
    ).wait_send()
    for copy in kv_out + kv_relay:
        copy.wait_send()


def write_out(*refs):
    half = len(refs) // 2
    sems = refs[-1]
    copies = [pltpu.make_async_copy(refs[i], refs[half + i], sems.at[i]) for i in range(half)]
    for copy in copies:
        copy.start()
    for copy in copies:
        copy.wait()


def on_device(expert_weights, kv_up_weight, owner_table, moved_experts):
    n, rows, columns = expert_weights.shape
    kv_rows, kv_columns = kv_up_weight.shape
    kv_all = kv_rows * Y_LO * CORE
    whole = n * rows
    vmem = pl.BlockSpec(memory_space=pltpu.VMEM)
    hbm = pl.BlockSpec(memory_space=pltpu.HBM)
    results = pl.pallas_call(
        kernel,
        out_shape=(
            jax.ShapeDtypeStruct((whole, columns), jnp.bfloat16),
            jax.ShapeDtypeStruct((1, whole // BLOCK), jnp.float32),
            jax.ShapeDtypeStruct((kv_all, kv_columns), jnp.bfloat16),
            jax.ShapeDtypeStruct((kv_all // BLOCK, kv_columns // BLOCK), jnp.float32),
        ),
        in_specs=[hbm] * 4,
        out_specs=(vmem, vmem, vmem, vmem),
        scratch_shapes=[
            pltpu.VMEM((n, rows, columns), jnp.bfloat16),
            pltpu.VMEM((whole, columns), jnp.bfloat16),
            pltpu.VMEM((whole, columns), jnp.bfloat16),
            pltpu.VMEM((kv_all, kv_columns), jnp.bfloat16),
            pltpu.VMEM((1, owner_table.shape[0]), jnp.int32),
            pltpu.VMEM((1, n), jnp.int32),
            pltpu.VMEM((8, 128), jnp.int32),
            pltpu.SMEM((8, 128), jnp.int32),
            pltpu.SemaphoreType.DMA((4,)),
            pltpu.SemaphoreType.DMA,
            pltpu.SemaphoreType.DMA((n,)),
            pltpu.SemaphoreType.DMA((2 * Y_LO,)),
            pltpu.SemaphoreType.DMA((Y_LO * CORE,)),
            pltpu.SemaphoreType.DMA,
        ],
        compiler_params=pltpu.CompilerParams(
            collective_id=0, has_side_effects=True, vmem_limit_bytes=40 << 20
        ),
    )(
        *(
            pltpu.with_memory_space_constraint(a, pltpu.HBM)
            for a in (expert_weights, kv_up_weight, owner_table.reshape(1, -1), moved_experts.reshape(1, -1))
        ),
    )
    values, scales, mla_values, mla_scales = pl.pallas_call(
        write_out,
        out_shape=tuple(jax.ShapeDtypeStruct(r.shape, r.dtype) for r in results),
        in_specs=[vmem] * 4,
        out_specs=(hbm,) * 4,
        scratch_shapes=[pltpu.SemaphoreType.DMA((4,))],
    )(*results)
    return (
        values.reshape(1, whole, columns),
        scales.reshape(1, whole // BLOCK, 1),
        mla_values,
        mla_scales,
    )


def solution(mesh):
    in_specs = (P(None, "expert", "fsdp"), P("fsdp", "expert"), P(), P())
    out_specs = (
        P("expert", None, "fsdp"),
        P("expert", None, "fsdp"),
        P(None, "expert"),
        P(None, "expert"),
    )
    return jax.shard_map(
        on_device, mesh=mesh, in_specs=in_specs, out_specs=out_specs, check_vma=False
    )
```

```python
import functools

import jax
import jax.numpy as jnp
from jax import lax
from jax.experimental import pallas as pl
from jax.experimental.pallas import tpu as pltpu
from jax.sharding import PartitionSpec as P

MESH = pl.DeviceIdType.MESH
BLOCK = 128
EPSILON = 1e-06
Y_HI, Z, X = 2, 8, 4
Y_LO, CORE = 4, 2
FORWARD = (4, 3, 5, 2, 6, 1, 7, 0)
GATHER_AT = 5


def own_order():
    return [(dz, dx) for dx in range(X) for dz in (4, 3, 5, 2, 6, 1, 7, 0) if dz or dx]


def kernel(
    x_hbm, kv_hbm, table_hbm, moved_hbm,
    values_ref, scales_ref, mla_values_ref, mla_scales_ref,
    x_ref, staged, relayed, landed, kv_landed, table_ref, moved_ref, rank_vmem, rank_smem,
    in_sem, own_send, y_send, relay_send, y_recv, recv_sem, kv_send, kv_recv, rank_sem,
):
    n = Y_HI * Z * X
    rows = x_ref.shape[1]
    me, fs = lax.axis_index("expert"), lax.axis_index("fsdp")
    y_hi, z, x = me // (Z * X), (me // X) % Z, me % X
    y_lo, core = fs // CORE, fs % CORE

    load_moved = pltpu.make_async_copy(moved_hbm, moved_ref, in_sem.at[2])
    load_moved.start()
    load_table = pltpu.make_async_copy(table_hbm, table_ref, in_sem.at[3])
    load_table.start()
    load_x = pltpu.make_async_copy(x_hbm, x_ref, in_sem.at[0])
    load_x.start()
    kv_rows = kv_hbm.shape[0]
    my_kv = kv_landed.at[pl.ds(pl.multiple_of(fs * kv_rows, kv_rows), kv_rows)]
    load_kv = pltpu.make_async_copy(kv_hbm, my_kv, in_sem.at[1])
    load_kv.start()

    here, there = y_hi * (Z * X), (1 - y_hi) * (Z * X)
    zs = [((z + d) % Z) * X for d in range(Z)]
    xs = [(x + d) % X for d in range(X)]
    partner = there + zs[0] + xs[0]
    fs_same = [((y_lo + d) % Y_LO) * CORE + core for d in range(Y_LO)]
    sibling = y_lo * CORE + 1 - core
    near = [(dz, dx) for dz in range(Z) for dx in range(X) if dz or dx]

    barrier = pltpu.get_barrier_semaphore()

    def greet(expert, fsdp):
        pl.semaphore_signal(barrier, inc=1, device_id=(expert, fsdp), device_id_type=MESH)

    greet(partner, fs)
    for dz, dx in near:
        greet(here + zs[dz] + xs[dx], fs)
    for d in range(1, Y_LO):
        greet(me, fs_same[d])
    greet(me, sibling)

    load_moved.wait()
    load_table.wait()
    lane = lax.broadcasted_iota(jnp.int32, (n, n), 1)
    row = lax.broadcasted_iota(jnp.int32, (n, n), 0)
    moved = jnp.sum(jnp.where(lane == row, moved_ref[...], 0), axis=1, keepdims=True)
    layer = lax.broadcasted_iota(jnp.int32, (n, table_ref.shape[1]), 1)
    owners = jnp.sum(jnp.where(layer == moved, table_ref[...], 0), axis=1, keepdims=True)
    wide = lax.broadcasted_iota(jnp.int32, (n, 128), 1)
    position = lax.broadcasted_iota(jnp.int32, (n, 128), 0)
    ranking = jnp.max(jnp.where(owners == wide, position, 0), axis=0, keepdims=True)
    rank_vmem[...] = jnp.broadcast_to(ranking, rank_vmem.shape)
    to_smem = pltpu.make_async_copy(rank_vmem, rank_smem, rank_sem)
    to_smem.start()
    to_smem.wait()
    load_x.wait()
    load_kv.wait()

    def stage(slot, owner):
        staged[pl.ds(slot * rows, rows), :] = x_ref[rank_smem[0, owner]]

    def chunk_copy(j):
        part = pl.ds(j * X * rows, X * rows)
        return pltpu.make_async_remote_copy(
            src_ref=staged.at[part], dst_ref=relayed.at[part], send_sem=y_send,
            recv_sem=y_recv.at[j], device_id=(partner, fs), device_id_type=MESH,
        )

    def block_copy(source, origin, dest, sem):
        to = pl.ds(pl.multiple_of(origin * rows, 16), rows)
        return pltpu.make_async_remote_copy(
            src_ref=source, dst_ref=landed.at[to], send_sem=sem,
            recv_sem=recv_sem.at[origin], device_id=(dest, fs), device_id_type=MESH,
        )

    def kv_copy(source, target, dev):
        part = kv_landed.at[pl.ds(pl.multiple_of(source * kv_rows, kv_rows), kv_rows)]
        return pltpu.make_async_remote_copy(
            src_ref=part, dst_ref=part, send_sem=kv_send.at[target], recv_sem=kv_recv.at[source],
            device_id=(me, dev), device_id_type=MESH,
        )

    def stage_chunk(j):
        for dx in range(X):
            stage(j * X + dx, there + zs[FORWARD[j]] + xs[dx])

    stage_chunk(0)
    pl.semaphore_wait(barrier, 1 + len(near) + Y_LO)
    for j in range(Z):
        if j:
            stage_chunk(j)
        chunk_copy(j).start()
    for i, (dz, dx) in enumerate(own_order()):
        dest = here + zs[dz] + xs[dx]
        stage(Z * X + i, dest)
        block_copy(staged.at[pl.ds((Z * X + i) * rows, rows)], me, dest, own_send).start()
    landed[pl.ds(pl.multiple_of(me * rows, 16), rows), :] = x_ref[rank_smem[0, me]]

    kv_out = [kv_copy(fs, 0, sibling)] + [kv_copy(fs, d, fs_same[d]) for d in range(1, Y_LO)]
    for j, dz in enumerate(FORWARD):
        chunk_copy(j).wait_recv()
        for dx in range(X):
            part = pl.ds((j * X + dx) * rows, rows)
            if dz or dx:
                block_copy(relayed.at[part], partner, here + zs[dz] + xs[dx], relay_send).start()
            else:
                landed[pl.ds(pl.multiple_of(partner * rows, 16), rows), :] = relayed[part, :]
        if j + 1 == GATHER_AT:
            for copy in kv_out:
                copy.start()

    kv_relay = []
    for d in range(1, Y_LO):
        source = fs_same[d]
        kv_copy(source, 0, source).wait_recv()
        copy = kv_copy(source, Y_LO - 1 + d, sibling)
        copy.start()
        kv_relay.append(copy)

    def scaled(block):
        block = block.astype(jnp.float32)
        top = jnp.max(jnp.max(jnp.abs(block), axis=0, keepdims=True), axis=1, keepdims=True)
        scale = top + EPSILON
        return (block * (1.0 / scale)).astype(jnp.bfloat16), scale

    pair = 2 * X
    blocks = pair * rows // BLOCK
    slots = lax.broadcasted_iota(jnp.int32, scales_ref.shape, 1)

    def one_group(half, k, scales):
        first = half + k * pair
        for s in range(pair):
            source = first + s

            @pl.when(jnp.logical_and(source != me, source != partner))
            def _():
                where = landed.at[pl.ds(pl.multiple_of(source * rows, 16), rows)]
                block_copy(where, source, sibling, own_send).wait_recv()

        for b in range(blocks):
            at = first // pair * blocks + b
            where = pl.ds(pl.multiple_of(at * BLOCK, BLOCK), BLOCK)
            values_ref[where, :], scale = scaled(landed[where, :])
            scales = jnp.where(slots == at, scale, scales)
        return scales

    def half_of_groups(half, scales):
        return lax.fori_loop(
            0, Z // 2, lambda k, kept: one_group(half, (z // 2 + 2 + k * 3) % (Z // 2), kept), scales
        )

    scales = half_of_groups(here, jnp.zeros(scales_ref.shape, jnp.float32))

    for d in range(Y_LO):
        source = ((y_lo + d) % Y_LO) * CORE + 1 - core
        kv_copy(source, 0, sibling).wait_recv()
    tall, across = mla_scales_ref.shape
    at = lax.broadcasted_iota(jnp.int32, (tall, across), 0) * across + lax.broadcasted_iota(jnp.int32, (tall, across), 1)
    mla_scales = jnp.zeros((tall, across), jnp.float32)
    for a in range(tall):
        for b in range(across):
            where = (pl.ds(a * BLOCK, BLOCK), pl.ds(b * BLOCK, BLOCK))
            mla_values_ref[where], scale = scaled(kv_landed[where])
            mla_scales = jnp.where(at == a * across + b, scale, mla_scales)
    mla_scales_ref[...] = mla_scales

    scales_ref[...] = half_of_groups(there, scales)

    def all_sent(sem, count):
        sent = staged.at[pl.ds(0, count * rows)]
        pltpu.make_async_remote_copy(
            src_ref=sent, dst_ref=sent, send_sem=sem, recv_sem=recv_sem.at[me],
            device_id=(partner, fs), device_id_type=MESH,
        ).wait_send()

    all_sent(y_send, Z * X)
    all_sent(own_send, Z * X - 1)
    all_sent(relay_send, Z * X - 1)
    for copy in kv_out + kv_relay:
        copy.wait_send()


def write_out(*refs):
    half = len(refs) // 2
    sems = refs[-1]
    copies = [pltpu.make_async_copy(refs[i], refs[half + i], sems.at[i]) for i in range(half)]
    for copy in copies:
        copy.start()
    for copy in copies:
        copy.wait()


def on_device(expert_weights, kv_up_weight, owner_table, moved_experts):
    n, rows, columns = expert_weights.shape
    kv_rows, kv_columns = kv_up_weight.shape
    kv_all = kv_rows * Y_LO * CORE
    whole = n * rows
    vmem = pl.BlockSpec(memory_space=pltpu.VMEM)
    hbm = pl.BlockSpec(memory_space=pltpu.HBM)
    results = pl.pallas_call(
        kernel,
        out_shape=(
            jax.ShapeDtypeStruct((whole, columns), jnp.bfloat16),
            jax.ShapeDtypeStruct((1, whole // BLOCK), jnp.float32),
            jax.ShapeDtypeStruct((kv_all, kv_columns), jnp.bfloat16),
            jax.ShapeDtypeStruct((kv_all // BLOCK, kv_columns // BLOCK), jnp.float32),
        ),
        in_specs=[hbm] * 4,
        out_specs=(vmem, vmem, vmem, vmem),
        scratch_shapes=[
            pltpu.VMEM((n, rows, columns), jnp.bfloat16),
            pltpu.VMEM((whole, columns), jnp.bfloat16),
            pltpu.VMEM((whole // Y_HI, columns), jnp.bfloat16),
            pltpu.VMEM((whole, columns), jnp.bfloat16),
            pltpu.VMEM((kv_all, kv_columns), jnp.bfloat16),
            pltpu.VMEM((1, owner_table.shape[0]), jnp.int32),
            pltpu.VMEM((1, n), jnp.int32),
            pltpu.VMEM((8, 128), jnp.int32),
            pltpu.SMEM((8, 128), jnp.int32),
            pltpu.SemaphoreType.DMA((4,)),
            pltpu.SemaphoreType.DMA,
            pltpu.SemaphoreType.DMA,
            pltpu.SemaphoreType.DMA,
            pltpu.SemaphoreType.DMA((Z,)),
            pltpu.SemaphoreType.DMA((n,)),
            pltpu.SemaphoreType.DMA((2 * Y_LO,)),
            pltpu.SemaphoreType.DMA((Y_LO * CORE,)),
            pltpu.SemaphoreType.DMA,
        ],
        compiler_params=pltpu.CompilerParams(
            collective_id=0, has_side_effects=True, vmem_limit_bytes=40 << 20
        ),
    )(
        *(
            pltpu.with_memory_space_constraint(a, pltpu.HBM)
            for a in (expert_weights, kv_up_weight, owner_table.reshape(1, -1), moved_experts.reshape(1, -1))
        ),
    )
    values, scales, mla_values, mla_scales = pl.pallas_call(
        write_out,
        out_shape=tuple(jax.ShapeDtypeStruct(r.shape, r.dtype) for r in results),
        in_specs=[vmem] * 4,
        out_specs=(hbm,) * 4,
        scratch_shapes=[pltpu.SemaphoreType.DMA((4,))],
    )(*results)
    return (
        values.reshape(1, whole, columns),
        scales.reshape(1, whole // BLOCK, 1),
        mla_values,
        mla_scales,
    )


def solution(mesh):
    in_specs = (P(None, "expert", "fsdp"), P("fsdp", "expert"), P(), P())
    out_specs = (
        P("expert", None, "fsdp"),
        P("expert", None, "fsdp"),
        P(None, "expert"),
        P(None, "expert"),
    )
    return jax.shard_map(
        on_device, mesh=mesh, in_specs=in_specs, out_specs=out_specs, check_vma=False
    )
```

```python
import functools

import jax
import jax.numpy as jnp
from jax import lax
from jax.experimental import pallas as pl
from jax.experimental.pallas import tpu as pltpu
from jax.sharding import PartitionSpec as P

MESH = pl.DeviceIdType.MESH
BLOCK = 128
EPSILON = 1e-06
Y_HI, Z, X = 2, 8, 4
Y_LO, CORE = 4, 2
FORWARD = (4, 3, 5, 2, 6, 1, 7, 0)
GATHER_AT = 5


def own_order():
    return [(dz, dx) for dx in range(X) for dz in (4, 3, 5, 2, 6, 1, 7, 0) if dz or dx]


def kernel(
    x_hbm, kv_hbm, table_hbm, moved_hbm,
    values_ref, scales_ref, mla_values_ref, mla_scales_ref,
    x_ref, staged, relayed, landed, kv_landed, table_ref, moved_ref, rank_vmem, rank_smem,
    in_sem, own_send, y_send, relay_send, y_recv, recv_sem, kv_send, kv_recv, rank_sem, ready,
):
    n = Y_HI * Z * X
    rows = x_ref.shape[1]
    me, fs = lax.axis_index("expert"), lax.axis_index("fsdp")
    y_hi, z, x = me // (Z * X), (me // X) % Z, me % X
    y_lo, core = fs // CORE, fs % CORE

    load_moved = pltpu.make_async_copy(moved_hbm, moved_ref, in_sem.at[2])
    load_moved.start()
    load_table = pltpu.make_async_copy(table_hbm, table_ref, in_sem.at[3])
    load_table.start()
    load_x = pltpu.make_async_copy(x_hbm, x_ref, in_sem.at[0])
    load_x.start()
    kv_rows = kv_hbm.shape[0]
    my_kv = kv_landed.at[pl.ds(pl.multiple_of(fs * kv_rows, kv_rows), kv_rows)]
    load_kv = pltpu.make_async_copy(kv_hbm, my_kv, in_sem.at[1])
    load_kv.start()

    here, there = y_hi * (Z * X), (1 - y_hi) * (Z * X)
    zs = [((z + d) % Z) * X for d in range(Z)]
    xs = [(x + d) % X for d in range(X)]
    partner = there + zs[0] + xs[0]
    fs_same = [((y_lo + d) % Y_LO) * CORE + core for d in range(Y_LO)]
    sibling = y_lo * CORE + 1 - core
    half = Z // 2
    upper = z // half
    planes = half * X
    low, high = here, here + planes
    mine, others = here + upper * planes, here + (1 - upper) * planes
    steps = [((z + d) % half) * X for d in range(half)]

    barrier = pltpu.get_barrier_semaphore()

    def greet(expert, fsdp):
        pl.semaphore_signal(barrier, inc=1, device_id=(expert, fsdp), device_id_type=MESH)

    greet(partner, fs)

    @pl.when(upper == 0)
    def _():
        for k in range(planes):
            greet(others + k, fs)

    for d in range(half):
        for dx in range(X):
            if d or dx:
                greet(mine + steps[d] + xs[dx], fs)
    for d in range(1, Y_LO):
        greet(me, fs_same[d])
    greet(me, sibling)

    load_moved.wait()
    load_table.wait()
    lane = lax.broadcasted_iota(jnp.int32, (n, n), 1)
    row = lax.broadcasted_iota(jnp.int32, (n, n), 0)
    moved = jnp.sum(jnp.where(lane == row, moved_ref[...], 0), axis=1, keepdims=True)
    layer = lax.broadcasted_iota(jnp.int32, (n, table_ref.shape[1]), 1)
    owners = jnp.sum(jnp.where(layer == moved, table_ref[...], 0), axis=1, keepdims=True)
    wide = lax.broadcasted_iota(jnp.int32, (n, 128), 1)
    position = lax.broadcasted_iota(jnp.int32, (n, 128), 0)
    ranking = jnp.max(jnp.where(owners == wide, position, 0), axis=0, keepdims=True)
    rank_vmem[...] = jnp.broadcast_to(ranking, rank_vmem.shape)
    to_smem = pltpu.make_async_copy(rank_vmem, rank_smem, rank_sem)
    to_smem.start()
    to_smem.wait()
    load_x.wait()
    load_kv.wait()

    def stage(slot, owner):
        staged[pl.ds(slot * rows, rows), :] = x_ref[rank_smem[0, owner]]

    def chunk_copy(j):
        part = pl.ds(j * X * rows, X * rows)
        return pltpu.make_async_remote_copy(
            src_ref=staged.at[part], dst_ref=relayed.at[part], send_sem=y_send,
            recv_sem=y_recv.at[j], device_id=(partner, fs), device_id_type=MESH,
        )

    def block_copy(source, origin, dest, sem):
        to = pl.ds(pl.multiple_of(origin * rows, 16), rows)
        return pltpu.make_async_remote_copy(
            src_ref=source, dst_ref=landed.at[to], send_sem=sem,
            recv_sem=recv_sem.at[origin], device_id=(dest, fs), device_id_type=MESH,
        )

    def kv_copy(source, target, dev):
        part = kv_landed.at[pl.ds(pl.multiple_of(source * kv_rows, kv_rows), kv_rows)]
        return pltpu.make_async_remote_copy(
            src_ref=part, dst_ref=part, send_sem=kv_send.at[target], recv_sem=kv_recv.at[source],
            device_id=(me, dev), device_id_type=MESH,
        )

    def stage_chunk(j):
        for dx in range(X):
            stage(j * X + dx, there + zs[FORWARD[j]] + xs[dx])

    stage_chunk(0)
    pl.semaphore_wait(barrier, planes + Y_LO + planes * upper)

    @pl.when(upper == 1)
    def _():
        for k in range(planes):
            pl.semaphore_signal(ready, inc=1, device_id=(others + k, fs), device_id_type=MESH)

    for j in range(Z):
        if j:
            stage_chunk(j)
        chunk_copy(j).start()

    def send_own(slot, dest):
        stage(slot, dest)
        block_copy(staged.at[pl.ds(slot * rows, rows)], me, dest, own_send).start()

    @pl.when(upper == 0)
    def _():
        slot = Z * X
        for first in (low, high):
            if first is high:
                pl.semaphore_wait(ready, planes)
            for dx in range(X):
                for d in (0, 2, 1, 3):
                    if d or dx or first is high:
                        send_own(slot, first + steps[d] + xs[dx])
                        slot += 1

    @pl.when(upper == 1)
    def _():
        for i, (dz, dx) in enumerate(own_order()):
            send_own(Z * X + i, here + zs[dz] + xs[dx])

    landed[pl.ds(pl.multiple_of(me * rows, 16), rows), :] = x_ref[rank_smem[0, me]]

    kv_out = [kv_copy(fs, 0, sibling)] + [kv_copy(fs, d, fs_same[d]) for d in range(1, Y_LO)]
    for j, dz in enumerate(FORWARD):
        chunk_copy(j).wait_recv()
        for dx in range(X):
            part = pl.ds((j * X + dx) * rows, rows)
            if dz or dx:
                block_copy(relayed.at[part], partner, here + zs[dz] + xs[dx], relay_send).start()
            else:
                landed[pl.ds(pl.multiple_of(partner * rows, 16), rows), :] = relayed[part, :]
        if j + 1 == GATHER_AT:
            for copy in kv_out:
                copy.start()

    kv_relay = []
    for d in range(1, Y_LO):
        source = fs_same[d]
        kv_copy(source, 0, source).wait_recv()
        copy = kv_copy(source, Y_LO - 1 + d, sibling)
        copy.start()
        kv_relay.append(copy)

    def scaled(block):
        block = block.astype(jnp.float32)
        top = jnp.max(jnp.max(jnp.abs(block), axis=0, keepdims=True), axis=1, keepdims=True)
        scale = top + EPSILON
        return (block * (1.0 / scale)).astype(jnp.bfloat16), scale

    pair = 2 * X
    blocks = pair * rows // BLOCK
    slots = lax.broadcasted_iota(jnp.int32, scales_ref.shape, 1)

    def one_group(side, k, scales):
        first = side + k * pair
        for s in range(pair):
            source = first + s

            @pl.when(jnp.logical_and(source != me, source != partner))
            def _():
                where = landed.at[pl.ds(pl.multiple_of(source * rows, 16), rows)]
                block_copy(where, source, sibling, own_send).wait_recv()

        for b in range(blocks):
            at = first // pair * blocks + b
            where = pl.ds(pl.multiple_of(at * BLOCK, BLOCK), BLOCK)
            values_ref[where, :], scale = scaled(landed[where, :])
            scales = jnp.where(slots == at, scale, scales)
        return scales

    def half_of_groups(side, scales):
        return lax.fori_loop(
            0, Z // 2, lambda k, kept: one_group(side, (z // 2 + 2 + k * 3) % (Z // 2), kept), scales
        )

    scales = half_of_groups(here, jnp.zeros(scales_ref.shape, jnp.float32))

    for d in range(Y_LO):
        source = ((y_lo + d) % Y_LO) * CORE + 1 - core
        kv_copy(source, 0, sibling).wait_recv()
    tall, across = mla_scales_ref.shape
    at = lax.broadcasted_iota(jnp.int32, (tall, across), 0) * across + lax.broadcasted_iota(jnp.int32, (tall, across), 1)
    mla_scales = jnp.zeros((tall, across), jnp.float32)
    for a in range(tall):
        for b in range(across):
            where = (pl.ds(a * BLOCK, BLOCK), pl.ds(b * BLOCK, BLOCK))
            mla_values_ref[where], scale = scaled(kv_landed[where])
            mla_scales = jnp.where(at == a * across + b, scale, mla_scales)
    mla_scales_ref[...] = mla_scales

    scales_ref[...] = half_of_groups(there, scales)

    def all_sent(sem, count):
        sent = staged.at[pl.ds(0, count * rows)]
        pltpu.make_async_remote_copy(
            src_ref=sent, dst_ref=sent, send_sem=sem, recv_sem=recv_sem.at[me],
            device_id=(partner, fs), device_id_type=MESH,
        ).wait_send()

    all_sent(y_send, Z * X)
    all_sent(own_send, Z * X - 1)
    all_sent(relay_send, Z * X - 1)
    for copy in kv_out + kv_relay:
        copy.wait_send()


def write_out(*refs):
    half = len(refs) // 2
    sems = refs[-1]
    copies = [pltpu.make_async_copy(refs[i], refs[half + i], sems.at[i]) for i in range(half)]
    for copy in copies:
        copy.start()
    for copy in copies:
        copy.wait()


def on_device(expert_weights, kv_up_weight, owner_table, moved_experts):
    n, rows, columns = expert_weights.shape
    kv_rows, kv_columns = kv_up_weight.shape
    kv_all = kv_rows * Y_LO * CORE
    whole = n * rows
    vmem = pl.BlockSpec(memory_space=pltpu.VMEM)
    hbm = pl.BlockSpec(memory_space=pltpu.HBM)
    results = pl.pallas_call(
        kernel,
        out_shape=(
            jax.ShapeDtypeStruct((whole, columns), jnp.bfloat16),
            jax.ShapeDtypeStruct((1, whole // BLOCK), jnp.float32),
            jax.ShapeDtypeStruct((kv_all, kv_columns), jnp.bfloat16),
            jax.ShapeDtypeStruct((kv_all // BLOCK, kv_columns // BLOCK), jnp.float32),
        ),
        in_specs=[hbm] * 4,
        out_specs=(vmem, vmem, vmem, vmem),
        scratch_shapes=[
            pltpu.VMEM((n, rows, columns), jnp.bfloat16),
            pltpu.VMEM((whole, columns), jnp.bfloat16),
            pltpu.VMEM((whole // Y_HI, columns), jnp.bfloat16),
            pltpu.VMEM((whole, columns), jnp.bfloat16),
            pltpu.VMEM((kv_all, kv_columns), jnp.bfloat16),
            pltpu.VMEM((1, owner_table.shape[0]), jnp.int32),
            pltpu.VMEM((1, n), jnp.int32),
            pltpu.VMEM((8, 128), jnp.int32),
            pltpu.SMEM((8, 128), jnp.int32),
            pltpu.SemaphoreType.DMA((4,)),
            pltpu.SemaphoreType.DMA,
            pltpu.SemaphoreType.DMA,
            pltpu.SemaphoreType.DMA,
            pltpu.SemaphoreType.DMA((Z,)),
            pltpu.SemaphoreType.DMA((n,)),
            pltpu.SemaphoreType.DMA((2 * Y_LO,)),
            pltpu.SemaphoreType.DMA((Y_LO * CORE,)),
            pltpu.SemaphoreType.DMA,
            pltpu.SemaphoreType.REGULAR,
        ],
        compiler_params=pltpu.CompilerParams(
            collective_id=0, has_side_effects=True, vmem_limit_bytes=40 << 20
        ),
    )(
        *(
            pltpu.with_memory_space_constraint(a, pltpu.HBM)
            for a in (expert_weights, kv_up_weight, owner_table.reshape(1, -1), moved_experts.reshape(1, -1))
        ),
    )
    values, scales, mla_values, mla_scales = pl.pallas_call(
        write_out,
        out_shape=tuple(jax.ShapeDtypeStruct(r.shape, r.dtype) for r in results),
        in_specs=[pl.BlockSpec(memory_space=pl.ANY)] * 4,
        out_specs=(hbm,) * 4,
        scratch_shapes=[pltpu.SemaphoreType.DMA((4,))],
        compiler_params=pltpu.CompilerParams(vmem_limit_bytes=1 << 20),
    )(*(pltpu.with_memory_space_constraint(r, pltpu.VMEM) for r in results))
    return (
        values.reshape(1, whole, columns),
        scales.reshape(1, whole // BLOCK, 1),
        mla_values,
        mla_scales,
    )


def solution(mesh):
    in_specs = (P(None, "expert", "fsdp"), P("fsdp", "expert"), P(), P())
    out_specs = (
        P("expert", None, "fsdp"),
        P("expert", None, "fsdp"),
        P(None, "expert"),
        P(None, "expert"),
    )
    return jax.shard_map(
        on_device, mesh=mesh, in_specs=in_specs, out_specs=out_specs, check_vma=False
    )
```

```python
import functools

import jax
import jax.numpy as jnp
from jax import lax
from jax.experimental import pallas as pl
from jax.experimental.pallas import tpu as pltpu
from jax.sharding import PartitionSpec as P

MESH = pl.DeviceIdType.MESH
BLOCK = 128
EPSILON = 1e-06
Y_HI, Z, X = 2, 8, 4
Y_LO, CORE = 4, 2
FORWARD = (4, 3, 5, 2, 6, 1, 7, 0)
IN_FLIGHT = 3
GATHER_AT = 5
SPREAD = (0, 2, 1, 3)


def kernel(
    x_hbm, kv_hbm, table_hbm, moved_hbm,
    values_ref, scales_ref, mla_values_ref, mla_scales_ref,
    x_ref, staged, relayed, landed, kv_landed, table_ref, moved_ref, rank_vmem, rank_smem,
    in_sem, own_send, y_send, relay_send, y_recv, recv_sem, kv_send, kv_recv, rank_sem, partner_ready, plane_ready, gather_ready,
):
    n = Y_HI * Z * X
    rows = x_ref.shape[1]
    me, fs = lax.axis_index("expert"), lax.axis_index("fsdp")
    y_hi, z, x = me // (Z * X), (me // X) % Z, me % X
    y_lo, core = fs // CORE, fs % CORE

    load_moved = pltpu.make_async_copy(moved_hbm, moved_ref, in_sem.at[2])
    load_moved.start()
    load_table = pltpu.make_async_copy(table_hbm, table_ref, in_sem.at[3])
    load_table.start()
    load_x = pltpu.make_async_copy(x_hbm, x_ref, in_sem.at[0])
    load_x.start()
    kv_rows = kv_hbm.shape[0]
    my_kv = kv_landed.at[pl.ds(pl.multiple_of(fs * kv_rows, kv_rows), kv_rows)]
    load_kv = pltpu.make_async_copy(kv_hbm, my_kv, in_sem.at[1])
    load_kv.start()

    here, there = y_hi * (Z * X), (1 - y_hi) * (Z * X)
    zs = [((z + d) % Z) * X for d in range(Z)]
    xs = [(x + d) % X for d in range(X)]
    partner = there + zs[0] + xs[0]
    fs_same = [((y_lo + d) % Y_LO) * CORE + core for d in range(Y_LO)]
    sibling = y_lo * CORE + 1 - core
    half = Z // 2
    planes = half * X
    index = z * X + x
    spread = [(z + d) % half for d in SPREAD]
    late = y_lo + y_hi * (Y_LO - 1 - 2 * y_lo)
    lates = [fs_same[d] // CORE + y_hi * (Y_LO - 1 - 2 * (fs_same[d] // CORE)) for d in range(Y_LO)]

    barrier = pltpu.get_barrier_semaphore()

    def signal(sem, expert, fsdp):
        pl.semaphore_signal(sem, inc=1, device_id=(expert, fsdp), device_id_type=MESH)

    def wait_for(sem, count):
        @pl.when(count > 0)
        def _():
            pl.semaphore_wait(sem, count)

    @pl.when(y_hi == 0)
    def _():
        signal(barrier, partner, fs)

    @pl.loop(index + 1, Z * X)
    def _(k):
        signal(barrier, here + k, fs)

    for d in range(1, Y_LO):

        @pl.when(lates[d] > late)
        def _():
            signal(barrier, me, fs_same[d])

    @pl.when(core == 0)
    def _():
        signal(barrier, me, sibling)

    wait_for(barrier, index + y_hi + late + core)

    @pl.when(y_hi == 1)
    def _():
        signal(partner_ready, partner, fs)

    load_moved.wait()
    load_table.wait()
    lane = lax.broadcasted_iota(jnp.int32, (n, n), 1)
    row = lax.broadcasted_iota(jnp.int32, (n, n), 0)
    moved = jnp.sum(jnp.where(lane == row, moved_ref[...], 0), axis=1, keepdims=True)
    layer = lax.broadcasted_iota(jnp.int32, (n, table_ref.shape[1]), 1)
    owners = jnp.sum(jnp.where(layer == moved, table_ref[...], 0), axis=1, keepdims=True)
    wide = lax.broadcasted_iota(jnp.int32, (n, 128), 1)
    position = lax.broadcasted_iota(jnp.int32, (n, 128), 0)
    ranking = jnp.max(jnp.where(owners == wide, position, 0), axis=0, keepdims=True)
    rank_vmem[...] = jnp.broadcast_to(ranking, rank_vmem.shape)
    to_smem = pltpu.make_async_copy(rank_vmem, rank_smem, rank_sem)
    to_smem.start()
    to_smem.wait()
    load_x.wait()
    load_kv.wait()

    def stage(slot, owner):
        staged[pl.ds(slot * rows, rows), :] = x_ref[rank_smem[0, owner]]

    def chunk_copy(j):
        part = pl.ds(j * X * rows, X * rows)
        return pltpu.make_async_remote_copy(
            src_ref=staged.at[part], dst_ref=relayed.at[part], send_sem=y_send,
            recv_sem=y_recv.at[j], device_id=(partner, fs), device_id_type=MESH,
        )

    def block_copy(source, origin, dest, sem):
        to = pl.ds(pl.multiple_of(origin * rows, 16), rows)
        return pltpu.make_async_remote_copy(
            src_ref=source, dst_ref=landed.at[to], send_sem=sem,
            recv_sem=recv_sem.at[origin], device_id=(dest, fs), device_id_type=MESH,
        )

    def kv_copy(source, target, dev):
        part = kv_landed.at[pl.ds(pl.multiple_of(source * kv_rows, kv_rows), kv_rows)]
        return pltpu.make_async_remote_copy(
            src_ref=part, dst_ref=part, send_sem=kv_send.at[target], recv_sem=kv_recv.at[source],
            device_id=(me, dev), device_id_type=MESH,
        )

    def stage_chunk(j):
        for dx in range(X):
            stage(j * X + dx, there + zs[FORWARD[j]] + xs[dx])

    for j in range(IN_FLIGHT):
        stage_chunk(j)
    wait_for(partner_ready, 1 - y_hi)
    for j in range(IN_FLIGHT):
        chunk_copy(j).start()

    @pl.loop(0, index)
    def _(k):
        signal(plane_ready.at[z], here + k, fs)

    for d in range(1, Y_LO):

        @pl.when(lates[d] < late)
        def _():
            signal(gather_ready, me, fs_same[d])

    @pl.when(core == 1)
    def _():
        signal(gather_ready, me, sibling)

    for j in range(IN_FLIGHT, Z):
        stage_chunk(j)

    def send_own(slot, plane, dx):
        dest = here + plane * X + xs[dx]
        stage(slot, dest)
        block_copy(staged.at[pl.ds(slot * rows, rows)], me, dest, own_send).start()

    @pl.when(z < half)
    def _():
        slot = Z * X
        wait_for(plane_ready.at[z], X - 1 - x)
        for dx in range(1, X):
            send_own(slot, z, dx)
            slot += 1
        for d in (1, 3, 2):
            plane = (z + d) % half

            @pl.when(plane > z)
            def _():
                pl.semaphore_wait(plane_ready.at[plane], X)

            for dx in range(X):
                send_own(slot, plane, dx)
                slot += 1
        for plane in range(half, Z):
            pl.semaphore_wait(plane_ready.at[plane], X)
        for dx in range(X):
            for plane in spread:
                send_own(slot, half + plane, dx)
                slot += 1

    @pl.when(z >= half)
    def _():
        slot = Z * X
        for dx in range(X):
            for plane in spread:
                send_own(slot, plane, dx)
                slot += 1
        wait_for(plane_ready.at[z], X - 1 - x)
        for plane in range(half + 1, Z):

            @pl.when(plane > z)
            def _():
                pl.semaphore_wait(plane_ready.at[plane], X)

        for dx in range(X):
            for plane in spread[1:]:
                send_own(slot, half + plane, dx)
                slot += 1
        for dx in range(1, X):
            send_own(slot, z, dx)
            slot += 1

    landed[pl.ds(pl.multiple_of(me * rows, 16), rows), :] = x_ref[rank_smem[0, me]]

    kv_out = [kv_copy(fs, 0, sibling)] + [kv_copy(fs, d, fs_same[d]) for d in range(1, Y_LO)]
    for j, dz in enumerate(FORWARD):
        chunk_copy(j).wait_recv()
        if j + IN_FLIGHT < Z:
            chunk_copy(j + IN_FLIGHT).start()
        for dx in range(X):
            part = pl.ds((j * X + dx) * rows, rows)
            if dz or dx:
                block_copy(relayed.at[part], partner, here + zs[dz] + xs[dx], relay_send).start()
            else:
                landed[pl.ds(pl.multiple_of(partner * rows, 16), rows), :] = relayed[part, :]
        if j + 1 == GATHER_AT:
            wait_for(gather_ready, Y_LO - late - core)
            for copy in kv_out:
                copy.start()

    kv_relay = []
    for d in range(1, Y_LO):
        source = fs_same[d]
        kv_copy(source, 0, source).wait_recv()
        copy = kv_copy(source, Y_LO - 1 + d, sibling)
        copy.start()
        kv_relay.append(copy)

    def scaled(block):
        block = block.astype(jnp.float32)
        top = jnp.max(jnp.max(jnp.abs(block), axis=0, keepdims=True), axis=1, keepdims=True)
        scale = top + EPSILON
        return (block * (1.0 / scale)).astype(jnp.bfloat16), scale

    pair = 2 * X
    blocks = pair * rows // BLOCK
    slots = lax.broadcasted_iota(jnp.int32, scales_ref.shape, 1)

    def one_group(side, k, scales):
        first = side + k * pair
        for s in range(pair):
            source = first + s

            @pl.when(jnp.logical_and(source != me, source != partner))
            def _():
                where = landed.at[pl.ds(pl.multiple_of(source * rows, 16), rows)]
                block_copy(where, source, sibling, own_send).wait_recv()

        for b in range(blocks):
            at = first // pair * blocks + b
            where = pl.ds(pl.multiple_of(at * BLOCK, BLOCK), BLOCK)
            values_ref[where, :], scale = scaled(landed[where, :])
            scales = jnp.where(slots == at, scale, scales)
        return scales

    def half_of_groups(side, scales):
        return lax.fori_loop(
            0, Z // 2, lambda k, kept: one_group(side, (z // 2 + 2 + k * 3) % (Z // 2), kept), scales
        )

    scales = half_of_groups(here, jnp.zeros(scales_ref.shape, jnp.float32))

    for d in range(Y_LO):
        source = ((y_lo + d) % Y_LO) * CORE + 1 - core
        kv_copy(source, 0, sibling).wait_recv()
    tall, across = mla_scales_ref.shape
    at = lax.broadcasted_iota(jnp.int32, (tall, across), 0) * across + lax.broadcasted_iota(jnp.int32, (tall, across), 1)
    mla_scales = jnp.zeros((tall, across), jnp.float32)
    for a in range(tall):
        for b in range(across):
            where = (pl.ds(a * BLOCK, BLOCK), pl.ds(b * BLOCK, BLOCK))
            mla_values_ref[where], scale = scaled(kv_landed[where])
            mla_scales = jnp.where(at == a * across + b, scale, mla_scales)
    mla_scales_ref[...] = mla_scales

    scales_ref[...] = half_of_groups(there, scales)

    def all_sent(sem, count):
        sent = staged.at[pl.ds(0, count * rows)]
        pltpu.make_async_remote_copy(
            src_ref=sent, dst_ref=sent, send_sem=sem, recv_sem=recv_sem.at[me],
            device_id=(partner, fs), device_id_type=MESH,
        ).wait_send()

    all_sent(y_send, Z * X)
    all_sent(own_send, Z * X - 1)
    all_sent(relay_send, Z * X - 1)
    for copy in kv_out + kv_relay:
        copy.wait_send()


def write_out(*refs):
    half = len(refs) // 2
    sems = refs[-1]
    copies = [pltpu.make_async_copy(refs[i], refs[half + i], sems.at[i]) for i in range(half)]
    for copy in copies:
        copy.start()
    for copy in copies:
        copy.wait()


def on_device(expert_weights, kv_up_weight, owner_table, moved_experts):
    n, rows, columns = expert_weights.shape
    kv_rows, kv_columns = kv_up_weight.shape
    kv_all = kv_rows * Y_LO * CORE
    whole = n * rows
    vmem = pl.BlockSpec(memory_space=pltpu.VMEM)
    hbm = pl.BlockSpec(memory_space=pltpu.HBM)
    results = pl.pallas_call(
        kernel,
        out_shape=(
            jax.ShapeDtypeStruct((whole, columns), jnp.bfloat16),
            jax.ShapeDtypeStruct((1, whole // BLOCK), jnp.float32),
            jax.ShapeDtypeStruct((kv_all, kv_columns), jnp.bfloat16),
            jax.ShapeDtypeStruct((kv_all // BLOCK, kv_columns // BLOCK), jnp.float32),
        ),
        in_specs=[hbm] * 4,
        out_specs=(vmem, vmem, vmem, vmem),
        scratch_shapes=[
            pltpu.VMEM((n, rows, columns), jnp.bfloat16),
            pltpu.VMEM((whole, columns), jnp.bfloat16),
            pltpu.VMEM((whole // Y_HI, columns), jnp.bfloat16),
            pltpu.VMEM((whole, columns), jnp.bfloat16),
            pltpu.VMEM((kv_all, kv_columns), jnp.bfloat16),
            pltpu.VMEM((1, owner_table.shape[0]), jnp.int32),
            pltpu.VMEM((1, n), jnp.int32),
            pltpu.VMEM((8, 128), jnp.int32),
            pltpu.SMEM((8, 128), jnp.int32),
            pltpu.SemaphoreType.DMA((4,)),
            pltpu.SemaphoreType.DMA,
            pltpu.SemaphoreType.DMA,
            pltpu.SemaphoreType.DMA,
            pltpu.SemaphoreType.DMA((Z,)),
            pltpu.SemaphoreType.DMA((n,)),
            pltpu.SemaphoreType.DMA((2 * Y_LO,)),
            pltpu.SemaphoreType.DMA((Y_LO * CORE,)),
            pltpu.SemaphoreType.DMA,
            pltpu.SemaphoreType.REGULAR,
            pltpu.SemaphoreType.REGULAR((Z,)),
            pltpu.SemaphoreType.REGULAR,
        ],
        compiler_params=pltpu.CompilerParams(
            collective_id=0, has_side_effects=True, vmem_limit_bytes=40 << 20
        ),
    )(
        *(
            pltpu.with_memory_space_constraint(a, pltpu.HBM)
            for a in (expert_weights, kv_up_weight, owner_table.reshape(1, -1), moved_experts.reshape(1, -1))
        ),
    )
    values, scales, mla_values, mla_scales = pl.pallas_call(
        write_out,
        out_shape=tuple(jax.ShapeDtypeStruct(r.shape, r.dtype) for r in results),
        in_specs=[pl.BlockSpec(memory_space=pl.ANY)] * 4,
        out_specs=(hbm,) * 4,
        scratch_shapes=[pltpu.SemaphoreType.DMA((4,))],
        compiler_params=pltpu.CompilerParams(vmem_limit_bytes=1 << 20),
    )(*(pltpu.with_memory_space_constraint(r, pltpu.VMEM) for r in results))
    return (
        values.reshape(1, whole, columns),
        scales.reshape(1, whole // BLOCK, 1),
        mla_values,
        mla_scales,
    )


def solution(mesh):
    in_specs = (P(None, "expert", "fsdp"), P("fsdp", "expert"), P(), P())
    out_specs = (
        P("expert", None, "fsdp"),
        P("expert", None, "fsdp"),
        P(None, "expert"),
        P(None, "expert"),
    )
    return jax.shard_map(
        on_device, mesh=mesh, in_specs=in_specs, out_specs=out_specs, check_vma=False
    )
```

```python
import functools

import jax
import jax.numpy as jnp
from jax import lax
from jax.experimental import pallas as pl
from jax.experimental.pallas import tpu as pltpu
from jax.sharding import PartitionSpec as P

MESH = pl.DeviceIdType.MESH
BLOCK = 128
EPSILON = 1e-06
Y_HI, Z, X = 2, 8, 4
Y_LO, CORE = 4, 2
FORWARD = (4, 3, 5, 2, 6, 1, 7, 0)
FORWARD_LAST = (4, 3, 1, 5, 2, 6, 7, 0)
IN_FLIGHT = 3
GATHER_AT = 5
SPREAD = (0, 2, 1, 3)


def kernel(
    x_hbm, kv_hbm, table_hbm, moved_hbm,
    values_ref, scales_ref, mla_values_ref, mla_scales_ref,
    x_ref, staged, relayed, landed, kv_landed, table_ref, moved_ref, rank_vmem, rank_smem,
    in_sem, own_send, y_send, relay_send, y_recv, recv_sem, kv_send, kv_recv, rank_sem, partner_ready, plane_ready, gather_ready,
):
    n = Y_HI * Z * X
    rows = x_ref.shape[1]
    me, fs = lax.axis_index("expert"), lax.axis_index("fsdp")
    y_hi, z, x = me // (Z * X), (me // X) % Z, me % X
    y_lo, core = fs // CORE, fs % CORE

    load_moved = pltpu.make_async_copy(moved_hbm, moved_ref, in_sem.at[2])
    load_moved.start()
    load_table = pltpu.make_async_copy(table_hbm, table_ref, in_sem.at[3])
    load_table.start()
    load_x = pltpu.make_async_copy(x_hbm, x_ref, in_sem.at[0])
    load_x.start()
    kv_rows = kv_hbm.shape[0]
    my_kv = kv_landed.at[pl.ds(pl.multiple_of(fs * kv_rows, kv_rows), kv_rows)]
    load_kv = pltpu.make_async_copy(kv_hbm, my_kv, in_sem.at[1])
    load_kv.start()

    here, there = y_hi * (Z * X), (1 - y_hi) * (Z * X)
    last = z // (Z - 1)
    forward = [((z + a + last * (b - a)) % Z) * X for a, b in zip(FORWARD, FORWARD_LAST)]
    xs = [(x + d) % X for d in range(X)]
    partner = there + z * X + x
    fs_same = [((y_lo + d) % Y_LO) * CORE + core for d in range(Y_LO)]
    sibling = y_lo * CORE + 1 - core
    half = Z // 2
    planes = half * X
    index = z * X + x
    spread = [(z + d) % half for d in SPREAD]
    late = y_lo + y_hi * (Y_LO - 1 - 2 * y_lo)
    lates = [fs_same[d] // CORE + y_hi * (Y_LO - 1 - 2 * (fs_same[d] // CORE)) for d in range(Y_LO)]

    barrier = pltpu.get_barrier_semaphore()

    def signal(sem, expert, fsdp):
        pl.semaphore_signal(sem, inc=1, device_id=(expert, fsdp), device_id_type=MESH)

    def wait_for(sem, count):
        @pl.when(count > 0)
        def _():
            pl.semaphore_wait(sem, count)

    @pl.when(y_hi == 0)
    def _():
        signal(barrier, partner, fs)

    @pl.loop(index + 1, Z * X)
    def _(k):
        signal(barrier, here + k, fs)

    for d in range(1, Y_LO):

        @pl.when(lates[d] > late)
        def _():
            signal(barrier, me, fs_same[d])

    @pl.when(core == 0)
    def _():
        signal(barrier, me, sibling)

    wait_for(barrier, index + y_hi + late + core)

    @pl.when(y_hi == 1)
    def _():
        signal(partner_ready, partner, fs)

    load_moved.wait()
    load_table.wait()
    lane = lax.broadcasted_iota(jnp.int32, (n, n), 1)
    row = lax.broadcasted_iota(jnp.int32, (n, n), 0)
    moved = jnp.sum(jnp.where(lane == row, moved_ref[...], 0), axis=1, keepdims=True)
    layer = lax.broadcasted_iota(jnp.int32, (n, table_ref.shape[1]), 1)
    owners = jnp.sum(jnp.where(layer == moved, table_ref[...], 0), axis=1, keepdims=True)
    wide = lax.broadcasted_iota(jnp.int32, (n, 128), 1)
    position = lax.broadcasted_iota(jnp.int32, (n, 128), 0)
    ranking = jnp.max(jnp.where(owners == wide, position, 0), axis=0, keepdims=True)
    rank_vmem[...] = jnp.broadcast_to(ranking, rank_vmem.shape)
    to_smem = pltpu.make_async_copy(rank_vmem, rank_smem, rank_sem)
    to_smem.start()
    to_smem.wait()
    load_x.wait()
    load_kv.wait()

    def stage(slot, owner):
        staged[pl.ds(slot * rows, rows), :] = x_ref[rank_smem[0, owner]]

    def chunk_copy(j):
        part = pl.ds(j * X * rows, X * rows)
        return pltpu.make_async_remote_copy(
            src_ref=staged.at[part], dst_ref=relayed.at[part], send_sem=y_send,
            recv_sem=y_recv.at[j], device_id=(partner, fs), device_id_type=MESH,
        )

    def block_copy(source, origin, dest, sem):
        to = pl.ds(pl.multiple_of(origin * rows, 16), rows)
        return pltpu.make_async_remote_copy(
            src_ref=source, dst_ref=landed.at[to], send_sem=sem,
            recv_sem=recv_sem.at[origin], device_id=(dest, fs), device_id_type=MESH,
        )

    def kv_copy(source, target, dev):
        part = kv_landed.at[pl.ds(pl.multiple_of(source * kv_rows, kv_rows), kv_rows)]
        return pltpu.make_async_remote_copy(
            src_ref=part, dst_ref=part, send_sem=kv_send.at[target], recv_sem=kv_recv.at[source],
            device_id=(me, dev), device_id_type=MESH,
        )

    def stage_chunk(j):
        for dx in range(X):
            stage(j * X + dx, there + forward[j] + xs[dx])

    for j in range(IN_FLIGHT):
        stage_chunk(j)
    wait_for(partner_ready, 1 - y_hi)
    for j in range(IN_FLIGHT):
        chunk_copy(j).start()

    @pl.loop(0, index)
    def _(k):
        signal(plane_ready.at[z], here + k, fs)

    for d in range(1, Y_LO):

        @pl.when(lates[d] < late)
        def _():
            signal(gather_ready, me, fs_same[d])

    @pl.when(core == 1)
    def _():
        signal(gather_ready, me, sibling)

    for j in range(IN_FLIGHT, Z):
        stage_chunk(j)

    def send_own(slot, plane, dx):
        dest = here + plane * X + xs[dx]
        stage(slot, dest)
        block_copy(staged.at[pl.ds(slot * rows, rows)], me, dest, own_send).start()

    @pl.when(z < half)
    def _():
        slot = Z * X
        wait_for(plane_ready.at[z], X - 1 - x)
        for dx in range(1, X):
            send_own(slot, z, dx)
            slot += 1
        for d in (1, 3, 2):
            plane = (z + d) % half

            @pl.when(plane > z)
            def _():
                pl.semaphore_wait(plane_ready.at[plane], X)

            for dx in range(X):
                send_own(slot, plane, dx)
                slot += 1
        for plane in range(half, Z):
            pl.semaphore_wait(plane_ready.at[plane], X)
        for dx in range(X):
            for plane in spread:
                send_own(slot, half + plane, dx)
                slot += 1

    @pl.when(z >= half)
    def _():
        slot = Z * X
        for dx in range(X):
            for plane in spread:
                send_own(slot, plane, dx)
                slot += 1
        wait_for(plane_ready.at[z], X - 1 - x)
        for plane in range(half + 1, Z):

            @pl.when(plane > z)
            def _():
                pl.semaphore_wait(plane_ready.at[plane], X)

        for dx in range(X):
            for plane in spread[1:]:
                send_own(slot, half + plane, dx)
                slot += 1
        for dx in range(1, X):
            send_own(slot, z, dx)
            slot += 1

    landed[pl.ds(pl.multiple_of(me * rows, 16), rows), :] = x_ref[rank_smem[0, me]]

    kv_out = [kv_copy(fs, 0, sibling)] + [kv_copy(fs, d, fs_same[d]) for d in range(1, Y_LO)]
    for j, dz in enumerate(FORWARD):
        chunk_copy(j).wait_recv()
        if j + IN_FLIGHT < Z:
            chunk_copy(j + IN_FLIGHT).start()
        for dx in range(X):
            part = pl.ds((j * X + dx) * rows, rows)
            if dz or dx:
                block_copy(relayed.at[part], partner, here + forward[j] + xs[dx], relay_send).start()
            else:
                landed[pl.ds(pl.multiple_of(partner * rows, 16), rows), :] = relayed[part, :]
        if j + 1 == GATHER_AT:
            wait_for(gather_ready, Y_LO - late - core)
            for copy in kv_out:
                copy.start()

    kv_relay = []
    for d in range(1, Y_LO):
        source = fs_same[d]
        kv_copy(source, 0, source).wait_recv()
        copy = kv_copy(source, Y_LO - 1 + d, sibling)
        copy.start()
        kv_relay.append(copy)

    def scaled(block):
        block = block.astype(jnp.float32)
        top = jnp.max(jnp.max(jnp.abs(block), axis=0, keepdims=True), axis=1, keepdims=True)
        scale = top + EPSILON
        return (block * (1.0 / scale)).astype(jnp.bfloat16), scale

    pair = 2 * X
    blocks = pair * rows // BLOCK
    slots = lax.broadcasted_iota(jnp.int32, scales_ref.shape, 1)

    def one_group(side, k, scales):
        first = side + k * pair
        for s in range(pair):
            source = first + s

            @pl.when(jnp.logical_and(source != me, source != partner))
            def _():
                where = landed.at[pl.ds(pl.multiple_of(source * rows, 16), rows)]
                block_copy(where, source, sibling, own_send).wait_recv()

        for b in range(blocks):
            at = first // pair * blocks + b
            where = pl.ds(pl.multiple_of(at * BLOCK, BLOCK), BLOCK)
            values_ref[where, :], scale = scaled(landed[where, :])
            scales = jnp.where(slots == at, scale, scales)
        return scales

    def half_of_groups(side, scales):
        return lax.fori_loop(
            0, Z // 2, lambda k, kept: one_group(side, (z // 2 + 2 + k * 3) % (Z // 2), kept), scales
        )

    scales = half_of_groups(here, jnp.zeros(scales_ref.shape, jnp.float32))

    for d in range(Y_LO):
        source = ((y_lo + d) % Y_LO) * CORE + 1 - core
        kv_copy(source, 0, sibling).wait_recv()
    tall, across = mla_scales_ref.shape
    at = lax.broadcasted_iota(jnp.int32, (tall, across), 0) * across + lax.broadcasted_iota(jnp.int32, (tall, across), 1)
    mla_scales = jnp.zeros((tall, across), jnp.float32)
    for a in range(tall):
        for b in range(across):
            where = (pl.ds(a * BLOCK, BLOCK), pl.ds(b * BLOCK, BLOCK))
            mla_values_ref[where], scale = scaled(kv_landed[where])
            mla_scales = jnp.where(at == a * across + b, scale, mla_scales)
    mla_scales_ref[...] = mla_scales

    scales_ref[...] = half_of_groups(there, scales)

    def all_sent(sem, count):
        sent = staged.at[pl.ds(0, count * rows)]
        pltpu.make_async_remote_copy(
            src_ref=sent, dst_ref=sent, send_sem=sem, recv_sem=recv_sem.at[me],
            device_id=(partner, fs), device_id_type=MESH,
        ).wait_send()

    all_sent(y_send, Z * X)
    all_sent(own_send, Z * X - 1)
    all_sent(relay_send, Z * X - 1)
    for copy in kv_out + kv_relay:
        copy.wait_send()


def write_out(*refs):
    half = len(refs) // 2
    sems = refs[-1]
    copies = [pltpu.make_async_copy(refs[i], refs[half + i], sems.at[i]) for i in range(half)]
    for copy in copies:
        copy.start()
    for copy in copies:
        copy.wait()


def on_device(expert_weights, kv_up_weight, owner_table, moved_experts):
    n, rows, columns = expert_weights.shape
    kv_rows, kv_columns = kv_up_weight.shape
    kv_all = kv_rows * Y_LO * CORE
    whole = n * rows
    vmem = pl.BlockSpec(memory_space=pltpu.VMEM)
    hbm = pl.BlockSpec(memory_space=pltpu.HBM)
    results = pl.pallas_call(
        kernel,
        out_shape=(
            jax.ShapeDtypeStruct((whole, columns), jnp.bfloat16),
            jax.ShapeDtypeStruct((1, whole // BLOCK), jnp.float32),
            jax.ShapeDtypeStruct((kv_all, kv_columns), jnp.bfloat16),
            jax.ShapeDtypeStruct((kv_all // BLOCK, kv_columns // BLOCK), jnp.float32),
        ),
        in_specs=[hbm] * 4,
        out_specs=(vmem, vmem, vmem, vmem),
        scratch_shapes=[
            pltpu.VMEM((n, rows, columns), jnp.bfloat16),
            pltpu.VMEM((whole, columns), jnp.bfloat16),
            pltpu.VMEM((whole // Y_HI, columns), jnp.bfloat16),
            pltpu.VMEM((whole, columns), jnp.bfloat16),
            pltpu.VMEM((kv_all, kv_columns), jnp.bfloat16),
            pltpu.VMEM((1, owner_table.shape[0]), jnp.int32),
            pltpu.VMEM((1, n), jnp.int32),
            pltpu.VMEM((8, 128), jnp.int32),
            pltpu.SMEM((8, 128), jnp.int32),
            pltpu.SemaphoreType.DMA((4,)),
            pltpu.SemaphoreType.DMA,
            pltpu.SemaphoreType.DMA,
            pltpu.SemaphoreType.DMA,
            pltpu.SemaphoreType.DMA((Z,)),
            pltpu.SemaphoreType.DMA((n,)),
            pltpu.SemaphoreType.DMA((2 * Y_LO,)),
            pltpu.SemaphoreType.DMA((Y_LO * CORE,)),
            pltpu.SemaphoreType.DMA,
            pltpu.SemaphoreType.REGULAR,
            pltpu.SemaphoreType.REGULAR((Z,)),
            pltpu.SemaphoreType.REGULAR,
        ],
        compiler_params=pltpu.CompilerParams(
            collective_id=0, has_side_effects=True, vmem_limit_bytes=40 << 20
        ),
    )(
        *(
            pltpu.with_memory_space_constraint(a, pltpu.HBM)
            for a in (expert_weights, kv_up_weight, owner_table.reshape(1, -1), moved_experts.reshape(1, -1))
        ),
    )
    values, scales, mla_values, mla_scales = pl.pallas_call(
        write_out,
        out_shape=tuple(jax.ShapeDtypeStruct(r.shape, r.dtype) for r in results),
        in_specs=[pl.BlockSpec(memory_space=pl.ANY)] * 4,
        out_specs=(hbm,) * 4,
        scratch_shapes=[pltpu.SemaphoreType.DMA((4,))],
        compiler_params=pltpu.CompilerParams(vmem_limit_bytes=1 << 20),
    )(*(pltpu.with_memory_space_constraint(r, pltpu.VMEM) for r in results))
    return (
        values.reshape(1, whole, columns),
        scales.reshape(1, whole // BLOCK, 1),
        mla_values,
        mla_scales,
    )


def solution(mesh):
    in_specs = (P(None, "expert", "fsdp"), P("fsdp", "expert"), P(), P())
    out_specs = (
        P("expert", None, "fsdp"),
        P("expert", None, "fsdp"),
        P(None, "expert"),
        P(None, "expert"),
    )
    return jax.shard_map(
        on_device, mesh=mesh, in_specs=in_specs, out_specs=out_specs, check_vma=False
    )
```

```python
import functools

import jax
import jax.numpy as jnp
from jax import lax
from jax.experimental import pallas as pl
from jax.experimental.pallas import tpu as pltpu
from jax.sharding import PartitionSpec as P

MESH = pl.DeviceIdType.MESH
BLOCK = 128
EPSILON = 1e-06
Y_HI, Z, X = 2, 8, 4
Y_LO, CORE = 4, 2
FORWARD = (4, 3, 5, 2, 6, 1, 7, 0)
FORWARD_LAST = (4, 3, 5, 1, 2, 6, 7, 0)
IN_FLIGHT = 3
GATHER_AT = 6
SPREAD = (0, 2, 1, 3)


def kernel(
    x_hbm, kv_hbm, table_hbm, moved_hbm,
    values_ref, scales_ref, mla_values_ref, mla_scales_ref,
    x_ref, staged, relayed, landed, kv_landed, table_ref, moved_ref, rank_vmem, rank_smem,
    in_sem, own_send, y_send, relay_send, y_recv, recv_sem, kv_send, kv_recv, rank_sem, partner_ready, plane_ready, gather_ready,
):
    n = Y_HI * Z * X
    rows = x_ref.shape[1]
    me, fs = lax.axis_index("expert"), lax.axis_index("fsdp")
    y_hi, z, x = me // (Z * X), (me // X) % Z, me % X
    y_lo, core = fs // CORE, fs % CORE

    load_moved = pltpu.make_async_copy(moved_hbm, moved_ref, in_sem.at[2])
    load_moved.start()
    load_table = pltpu.make_async_copy(table_hbm, table_ref, in_sem.at[3])
    load_table.start()
    load_x = pltpu.make_async_copy(x_hbm, x_ref, in_sem.at[0])
    load_x.start()
    kv_rows = kv_hbm.shape[0]
    my_kv = kv_landed.at[pl.ds(pl.multiple_of(fs * kv_rows, kv_rows), kv_rows)]
    load_kv = pltpu.make_async_copy(kv_hbm, my_kv, in_sem.at[1])
    load_kv.start()

    here, there = y_hi * (Z * X), (1 - y_hi) * (Z * X)
    last = z // (Z - 1)
    forward = [((z + a + last * (b - a)) % Z) * X for a, b in zip(FORWARD, FORWARD_LAST)]
    xs = [(x + d) % X for d in range(X)]
    partner = there + z * X + x
    fs_same = [((y_lo + d) % Y_LO) * CORE + core for d in range(Y_LO)]
    sibling = y_lo * CORE + 1 - core
    half = Z // 2
    planes = half * X
    index = z * X + x
    spread = [(z + d) % half for d in SPREAD]
    late = y_lo + y_hi * (Y_LO - 1 - 2 * y_lo)
    lates = [fs_same[d] // CORE + y_hi * (Y_LO - 1 - 2 * (fs_same[d] // CORE)) for d in range(Y_LO)]

    barrier = pltpu.get_barrier_semaphore()

    def signal(sem, expert, fsdp):
        pl.semaphore_signal(sem, inc=1, device_id=(expert, fsdp), device_id_type=MESH)

    def wait_for(sem, count):
        @pl.when(count > 0)
        def _():
            pl.semaphore_wait(sem, count)

    @pl.when(y_hi == 0)
    def _():
        signal(barrier, partner, fs)

    @pl.loop(index + 1, Z * X)
    def _(k):
        signal(barrier, here + k, fs)

    for d in range(1, Y_LO):

        @pl.when(lates[d] > late)
        def _():
            signal(barrier, me, fs_same[d])

    @pl.when(core == 0)
    def _():
        signal(barrier, me, sibling)

    wait_for(barrier, index + y_hi + late + core)

    @pl.when(y_hi == 1)
    def _():
        signal(partner_ready, partner, fs)

    load_moved.wait()
    load_table.wait()
    lane = lax.broadcasted_iota(jnp.int32, (n, n), 1)
    row = lax.broadcasted_iota(jnp.int32, (n, n), 0)
    moved = jnp.sum(jnp.where(lane == row, moved_ref[...], 0), axis=1, keepdims=True)
    layer = lax.broadcasted_iota(jnp.int32, (n, table_ref.shape[1]), 1)
    owners = jnp.sum(jnp.where(layer == moved, table_ref[...], 0), axis=1, keepdims=True)
    wide = lax.broadcasted_iota(jnp.int32, (n, 128), 1)
    position = lax.broadcasted_iota(jnp.int32, (n, 128), 0)
    ranking = jnp.max(jnp.where(owners == wide, position, 0), axis=0, keepdims=True)
    rank_vmem[...] = jnp.broadcast_to(ranking, rank_vmem.shape)
    to_smem = pltpu.make_async_copy(rank_vmem, rank_smem, rank_sem)
    to_smem.start()
    to_smem.wait()
    load_x.wait()
    load_kv.wait()

    def stage(slot, owner):
        staged[pl.ds(slot * rows, rows), :] = x_ref[rank_smem[0, owner]]

    def chunk_copy(j):
        part = pl.ds(j * X * rows, X * rows)
        return pltpu.make_async_remote_copy(
            src_ref=staged.at[part], dst_ref=relayed.at[part], send_sem=y_send,
            recv_sem=y_recv.at[j], device_id=(partner, fs), device_id_type=MESH,
        )

    def block_copy(source, origin, dest, sem):
        to = pl.ds(pl.multiple_of(origin * rows, 16), rows)
        return pltpu.make_async_remote_copy(
            src_ref=source, dst_ref=landed.at[to], send_sem=sem,
            recv_sem=recv_sem.at[origin], device_id=(dest, fs), device_id_type=MESH,
        )

    def kv_copy(source, target, dev):
        part = kv_landed.at[pl.ds(pl.multiple_of(source * kv_rows, kv_rows), kv_rows)]
        return pltpu.make_async_remote_copy(
            src_ref=part, dst_ref=part, send_sem=kv_send.at[target], recv_sem=kv_recv.at[source],
            device_id=(me, dev), device_id_type=MESH,
        )

    def stage_chunk(j):
        for dx in range(X):
            stage(j * X + dx, there + forward[j] + xs[dx])

    for j in range(IN_FLIGHT):
        stage_chunk(j)
    wait_for(partner_ready, 1 - y_hi)
    for j in range(IN_FLIGHT):
        chunk_copy(j).start()

    @pl.loop(0, index)
    def _(k):
        signal(plane_ready.at[z], here + k, fs)

    for d in range(1, Y_LO):

        @pl.when(lates[d] < late)
        def _():
            signal(gather_ready, me, fs_same[d])

    @pl.when(core == 1)
    def _():
        signal(gather_ready, me, sibling)

    for j in range(IN_FLIGHT, Z):
        stage_chunk(j)

    def send_own(slot, plane, dx):
        dest = here + plane * X + xs[dx]
        stage(slot, dest)
        block_copy(staged.at[pl.ds(slot * rows, rows)], me, dest, own_send).start()

    @pl.when(z < half)
    def _():
        slot = Z * X
        wait_for(plane_ready.at[z], X - 1 - x)
        for dx in range(1, X):
            send_own(slot, z, dx)
            slot += 1
        for d in (1, 3, 2):
            plane = (z + d) % half

            @pl.when(plane > z)
            def _():
                pl.semaphore_wait(plane_ready.at[plane], X)

            for dx in range(X):
                send_own(slot, plane, dx)
                slot += 1
        for plane in range(half, Z):
            pl.semaphore_wait(plane_ready.at[plane], X)
        for dx in range(X):
            for plane in spread:
                send_own(slot, half + plane, dx)
                slot += 1

    @pl.when(z >= half)
    def _():
        slot = Z * X
        for dx in range(X):
            for plane in spread:
                send_own(slot, plane, dx)
                slot += 1
        wait_for(plane_ready.at[z], X - 1 - x)
        for plane in range(half + 1, Z):

            @pl.when(plane > z)
            def _():
                pl.semaphore_wait(plane_ready.at[plane], X)

        for dx in range(X):
            for plane in spread[1:]:
                send_own(slot, half + plane, dx)
                slot += 1
        for dx in range(1, X):
            send_own(slot, z, dx)
            slot += 1

    landed[pl.ds(pl.multiple_of(me * rows, 16), rows), :] = x_ref[rank_smem[0, me]]

    kv_out = [kv_copy(fs, 0, sibling)] + [kv_copy(fs, d, fs_same[d]) for d in range(1, Y_LO)]
    for j, dz in enumerate(FORWARD):
        chunk_copy(j).wait_recv()
        if j + IN_FLIGHT < Z:
            chunk_copy(j + IN_FLIGHT).start()
        for dx in range(X):
            part = pl.ds((j * X + dx) * rows, rows)
            if dz or dx:
                block_copy(relayed.at[part], partner, here + forward[j] + xs[dx], relay_send).start()
            else:
                landed[pl.ds(pl.multiple_of(partner * rows, 16), rows), :] = relayed[part, :]
        if j + 1 == GATHER_AT:
            wait_for(gather_ready, Y_LO - late - core)
            for copy in kv_out:
                copy.start()

    kv_relay = []
    for d in range(1, Y_LO):
        source = fs_same[d]
        kv_copy(source, 0, source).wait_recv()
        copy = kv_copy(source, Y_LO - 1 + d, sibling)
        copy.start()
        kv_relay.append(copy)

    def scaled(block):
        block = block.astype(jnp.float32)
        top = jnp.max(jnp.max(jnp.abs(block), axis=0, keepdims=True), axis=1, keepdims=True)
        scale = top + EPSILON
        return (block * (1.0 / scale)).astype(jnp.bfloat16), scale

    pair = 2 * X
    blocks = pair * rows // BLOCK
    slots = lax.broadcasted_iota(jnp.int32, scales_ref.shape, 1)

    def one_group(side, k, scales):
        first = side + k * pair
        for s in range(pair):
            source = first + s

            @pl.when(jnp.logical_and(source != me, source != partner))
            def _():
                where = landed.at[pl.ds(pl.multiple_of(source * rows, 16), rows)]
                block_copy(where, source, sibling, own_send).wait_recv()

        for b in range(blocks):
            at = first // pair * blocks + b
            where = pl.ds(pl.multiple_of(at * BLOCK, BLOCK), BLOCK)
            values_ref[where, :], scale = scaled(landed[where, :])
            scales = jnp.where(slots == at, scale, scales)
        return scales

    def half_of_groups(side, scales):
        return lax.fori_loop(
            0, Z // 2, lambda k, kept: one_group(side, (z // 2 + 2 + k * 3) % (Z // 2), kept), scales
        )

    scales = half_of_groups(here, jnp.zeros(scales_ref.shape, jnp.float32))

    for d in range(Y_LO):
        source = ((y_lo + d) % Y_LO) * CORE + 1 - core
        kv_copy(source, 0, sibling).wait_recv()
    tall, across = mla_scales_ref.shape
    at = lax.broadcasted_iota(jnp.int32, (tall, across), 0) * across + lax.broadcasted_iota(jnp.int32, (tall, across), 1)
    mla_scales = jnp.zeros((tall, across), jnp.float32)
    for a in range(tall):
        for b in range(across):
            where = (pl.ds(a * BLOCK, BLOCK), pl.ds(b * BLOCK, BLOCK))
            mla_values_ref[where], scale = scaled(kv_landed[where])
            mla_scales = jnp.where(at == a * across + b, scale, mla_scales)
    mla_scales_ref[...] = mla_scales

    scales_ref[...] = half_of_groups(there, scales)

    def all_sent(sem, count):
        sent = staged.at[pl.ds(0, count * rows)]
        pltpu.make_async_remote_copy(
            src_ref=sent, dst_ref=sent, send_sem=sem, recv_sem=recv_sem.at[me],
            device_id=(partner, fs), device_id_type=MESH,
        ).wait_send()

    all_sent(y_send, Z * X)
    all_sent(own_send, Z * X - 1)
    all_sent(relay_send, Z * X - 1)
    for copy in kv_out + kv_relay:
        copy.wait_send()


def write_out(*refs):
    half = len(refs) // 2
    sems = refs[-1]
    copies = [pltpu.make_async_copy(refs[i], refs[half + i], sems.at[i]) for i in range(half)]
    for copy in copies:
        copy.start()
    for copy in copies:
        copy.wait()


def on_device(expert_weights, kv_up_weight, owner_table, moved_experts):
    n, rows, columns = expert_weights.shape
    kv_rows, kv_columns = kv_up_weight.shape
    kv_all = kv_rows * Y_LO * CORE
    whole = n * rows
    vmem = pl.BlockSpec(memory_space=pltpu.VMEM)
    hbm = pl.BlockSpec(memory_space=pltpu.HBM)
    results = pl.pallas_call(
        kernel,
        out_shape=(
            jax.ShapeDtypeStruct((whole, columns), jnp.bfloat16),
            jax.ShapeDtypeStruct((1, whole // BLOCK), jnp.float32),
            jax.ShapeDtypeStruct((kv_all, kv_columns), jnp.bfloat16),
            jax.ShapeDtypeStruct((kv_all // BLOCK, kv_columns // BLOCK), jnp.float32),
        ),
        in_specs=[hbm] * 4,
        out_specs=(vmem, vmem, vmem, vmem),
        scratch_shapes=[
            pltpu.VMEM((n, rows, columns), jnp.bfloat16),
            pltpu.VMEM((whole, columns), jnp.bfloat16),
            pltpu.VMEM((whole // Y_HI, columns), jnp.bfloat16),
            pltpu.VMEM((whole, columns), jnp.bfloat16),
            pltpu.VMEM((kv_all, kv_columns), jnp.bfloat16),
            pltpu.VMEM((1, owner_table.shape[0]), jnp.int32),
            pltpu.VMEM((1, n), jnp.int32),
            pltpu.VMEM((8, 128), jnp.int32),
            pltpu.SMEM((8, 128), jnp.int32),
            pltpu.SemaphoreType.DMA((4,)),
            pltpu.SemaphoreType.DMA,
            pltpu.SemaphoreType.DMA,
            pltpu.SemaphoreType.DMA,
            pltpu.SemaphoreType.DMA((Z,)),
            pltpu.SemaphoreType.DMA((n,)),
            pltpu.SemaphoreType.DMA((2 * Y_LO,)),
            pltpu.SemaphoreType.DMA((Y_LO * CORE,)),
            pltpu.SemaphoreType.DMA,
            pltpu.SemaphoreType.REGULAR,
            pltpu.SemaphoreType.REGULAR((Z,)),
            pltpu.SemaphoreType.REGULAR,
        ],
        compiler_params=pltpu.CompilerParams(
            collective_id=0, has_side_effects=True, vmem_limit_bytes=40 << 20
        ),
    )(
        *(
            pltpu.with_memory_space_constraint(a, pltpu.HBM)
            for a in (expert_weights, kv_up_weight, owner_table.reshape(1, -1), moved_experts.reshape(1, -1))
        ),
    )
    values, scales, mla_values, mla_scales = pl.pallas_call(
        write_out,
        out_shape=tuple(jax.ShapeDtypeStruct(r.shape, r.dtype) for r in results),
        in_specs=[pl.BlockSpec(memory_space=pl.ANY)] * 4,
        out_specs=(hbm,) * 4,
        scratch_shapes=[pltpu.SemaphoreType.DMA((4,))],
        compiler_params=pltpu.CompilerParams(vmem_limit_bytes=1 << 20),
    )(*(pltpu.with_memory_space_constraint(r, pltpu.VMEM) for r in results))
    return (
        values.reshape(1, whole, columns),
        scales.reshape(1, whole // BLOCK, 1),
        mla_values,
        mla_scales,
    )


def solution(mesh):
    in_specs = (P(None, "expert", "fsdp"), P("fsdp", "expert"), P(), P())
    out_specs = (
        P("expert", None, "fsdp"),
        P("expert", None, "fsdp"),
        P(None, "expert"),
        P(None, "expert"),
    )
    return jax.shard_map(
        on_device, mesh=mesh, in_specs=in_specs, out_specs=out_specs, check_vma=False
    )
```
